32 devices in a mesh: grp: 2 (over core), vocab: 4 (over z), tok: 4 (over y, x).
Axes of the slice: x: 2, y: 2, z: 4, core: 2. Of those that a mesh axis runs over, the one named last changes fastest.
Arguments:
- teacher_hidden: bfloat16 [512, 16384], P(('grp', 'vocab'), 'tok'), may hold values from -1000 to 1000
- student_hidden: bfloat16 [512, 8192], P(('grp', 'vocab'), 'tok'), may hold values from -1000 to 1000
- teacher_gain: float32 [16384], P('tok'), may hold values from 0.5 to 1.5
- student_gain: float32 [8192], P('tok'), may hold values from 0.5 to 1.5
- teacher_head: bfloat16 [65536, 16384], P(('grp', 'vocab'), 'tok'), may hold values from -64 to 64
- student_head: bfloat16 [65536, 8192], P(('grp', 'vocab'), 'tok'), may hold values from -64 to 64
- target_ids: int32 [512], replicated, may hold values from 0 to 65535
Outputs:
- loss: float32 [], replicated
- hidden_grad: bfloat16 [512, 8192], P(('grp', 'vocab'), 'tok')
The draws below stay inside these ranges and needn't reach their ends.
All inputs are finite; a program needn't handle non-finite values.
Results may differ from the reference program's by a relative error of at most 0.0039.
Values may be sent and summed in bfloat16 or wider, within the bound.
No kernel may reach another device: no remote copies, remote signals or barrier semaphores. Data moves between devices by JAX's collectives and lax.ppermute only.
A program may use at most 320 MiB of HBM per device.

```python
import math
import jax
import jax.numpy as jnp
import numpy as np
from jax import lax

DT = 16384
DS = 8192
VOCAB = 65536
TOKENS = 512


def draw_teacher_hidden(key, part):
    key = jax.random.fold_in(key, 11)
    key_list = jax.random.split(key, 4)
    column_scale = jnp.exp(jax.random.uniform(key_list[0], (1, DT), jnp.float32, 0.0, math.log(10.0)))
    row_scale = jnp.exp(jax.random.uniform(key_list[1], (TOKENS, 1), jnp.float32, 0.0, math.log(10.0)))
    values = jax.random.normal(key_list[3], (TOKENS, DT), jnp.float32) * row_scale * column_scale
    return jnp.clip(values, -1000.0, 1000.0).astype(jnp.bfloat16)


def draw_student_hidden(key, part):
    key = jax.random.fold_in(key, 12)
    key_list = jax.random.split(key, 4)
    column_scale = jnp.exp(jax.random.uniform(key_list[0], (1, DS), jnp.float32, 0.0, math.log(10.0)))
    row_scale = jnp.exp(jax.random.uniform(key_list[1], (TOKENS, 1), jnp.float32, 0.0, math.log(10.0)))
    values = jax.random.normal(key_list[3], (TOKENS, DS), jnp.float32) * row_scale * column_scale
    return jnp.clip(values, -1000.0, 1000.0).astype(jnp.bfloat16)


def draw_teacher_head(key, part):
    key = jax.random.fold_in(key, 13)
    weights = jax.random.normal(key, (VOCAB, DT), jnp.float32) * (3.0 / math.sqrt(DT))
    return jnp.clip(weights, -64.0, 64.0).astype(jnp.bfloat16)


def draw_student_head(key, part):
    key = jax.random.fold_in(key, 14)
    weights = jax.random.normal(key, (VOCAB, DS), jnp.float32) * (3.0 / math.sqrt(DS))
    return jnp.clip(weights, -64.0, 64.0).astype(jnp.bfloat16)


def set_ends(result, rng, smallest, high):
    extent = result.shape
    index_at = [jax.random.randint(jax.random.fold_in(rng, axis), (), 0, extent[axis]) for axis in range(len(extent))]
    result = result.at[tuple(index_at)].set(smallest)
    longest = extent.index(max(extent))
    index_at[longest] = (index_at[longest] + 1) % extent[longest]
    return result.at[tuple(index_at)].set(high)


def cumulative_ranks(count, slope):
    portions = [(1 << 20) // math.isqrt(grade ** slope) + 1 for grade in range(1, count + 1)]
    spread = 1 + sum(portions) // (1 << 30)
    return np.cumsum(np.array([max(1, weight // spread) for weight in portions]))


def ranked(key, extent, count, skew):
    table = cumulative_ranks(count, skew)
    lot = jax.random.randint(jax.random.fold_in(key, 1), extent, 0, int(table[count - 1]))
    grade = jnp.searchsorted(jnp.asarray(table, jnp.int32), lot, side="right")
    return jax.random.permutation(jax.random.fold_in(key, 2), count)[grade].astype(jnp.int32)


def setup_inputs(seed: int = 0) -> dict:
    streams_of = jax.random.split(jax.random.key(seed), 8)
    teacher_hidden = draw_teacher_hidden(jax.random.fold_in(streams_of[7], 71), 0)
    student_hidden = draw_student_hidden(jax.random.fold_in(streams_of[7], 71), 0)
    teacher_gain = jnp.clip(1.0 + 0.1 * jax.random.normal(streams_of[2], (DT,), jnp.float32), 0.5, 1.5)
    student_gain = jnp.clip(1.0 + 0.1 * jax.random.normal(streams_of[3], (DS,), jnp.float32), 0.5, 1.5)
    teacher_head = draw_teacher_head(jax.random.fold_in(streams_of[7], 71), 0)
    student_head = draw_student_head(jax.random.fold_in(streams_of[7], 71), 0)
    target_ids = set_ends(ranked(streams_of[6], (TOKENS,), VOCAB, 2), jax.random.fold_in(streams_of[6], 3), 0, VOCAB - 1).astype(jnp.int32)
    return dict(teacher_hidden=teacher_hidden, student_hidden=student_hidden, teacher_gain=teacher_gain, student_gain=student_gain, teacher_head=teacher_head, student_head=student_head, target_ids=target_ids)


heat_divisor = 2.0
blend_fraction = 0.5
objective_scale_factor = 1024.0
epsilon = 1e-05

def head_logits(hidden, gain, head, features):
    widened = hidden.astype(jnp.float32)
    weighted = (widened * gain).astype(jnp.bfloat16)
    inverse = lax.rsqrt(lax.optimization_barrier(jnp.sum(widened * widened, axis=1)) / features + epsilon)
    logits = jnp.dot(weighted, head.T, preferred_element_type=jnp.float32) * inverse[:, None]
    return (logits, inverse)

def reference(teacher_hidden, student_hidden, teacher_gain, student_gain, teacher_head, student_head, target_ids):
    mentor_score_table, teacher_inv = head_logits(teacher_hidden, teacher_gain, teacher_head, DT)
    learner_score_table, student_inv = head_logits(student_hidden, student_gain, student_head, DS)
    mentor_warmed_scores = mentor_score_table / heat_divisor
    score_gap = (mentor_score_table - learner_score_table) / heat_divisor
    mentor_example_peak = lax.optimization_barrier(jnp.max(mentor_warmed_scores, axis=1))
    mentor_power = jnp.exp(mentor_warmed_scores - mentor_example_peak[:, None])
    mentor_power_total = lax.optimization_barrier(jnp.sum(mentor_power, axis=1))
    likelihood_penalty_total = lax.optimization_barrier(jnp.sum(mentor_power * score_gap, axis=1))
    learner_example_peak = lax.optimization_barrier(jnp.max(learner_score_table, axis=1))
    warmed_power = jnp.exp((learner_score_table - learner_example_peak[:, None]) / heat_divisor)
    warmed_power_total = lax.optimization_barrier(jnp.sum(warmed_power, axis=1))
    bare_power = jnp.exp(learner_score_table - learner_example_peak[:, None])
    bare_power_total = lax.optimization_barrier(jnp.sum(bare_power, axis=1))
    columns = jnp.arange(VOCAB, dtype=jnp.int32)
    label_hits = target_ids.astype(jnp.int32)[:, None] == columns[None, :]
    label_score_entry = lax.optimization_barrier(jnp.sum(jnp.where(label_hits, learner_score_table, 0.0), axis=1))
    objective_by_example = blend_fraction * heat_divisor ** 2 * (likelihood_penalty_total / mentor_power_total - mentor_example_peak - jnp.log(mentor_power_total) + learner_example_peak / heat_divisor + jnp.log(warmed_power_total)) + (1.0 - blend_fraction) * (learner_example_peak + jnp.log(bare_power_total) - label_score_entry)
    loss = jnp.sum(objective_by_example) / TOKENS
    learner_score_slope = (objective_scale_factor * (blend_fraction * heat_divisor * (warmed_power / warmed_power_total[:, None] - mentor_power / mentor_power_total[:, None]) + (1.0 - blend_fraction) * (bare_power / bare_power_total[:, None] - label_hits.astype(jnp.float32)))).astype(jnp.bfloat16)
    norm_grad = jnp.dot(learner_score_slope, student_head, preferred_element_type=jnp.float32)
    widened = student_hidden.astype(jnp.float32)
    inner = lax.optimization_barrier(jnp.sum(student_gain * norm_grad * widened, axis=1))
    hidden_grad = (student_inv[:, None] * student_gain * norm_grad - widened * (student_inv ** 3 * inner / DS)[:, None]).astype(jnp.bfloat16)
    return (loss, hidden_grad)
```

```python
import functools
import jax
import jax.numpy as jnp
from jax import lax
from jax.experimental import pallas as pl
from jax.experimental.pallas import tpu as pltpu
from jax.sharding import PartitionSpec as P

heat = 2.0
blend = 0.5
grad_scale = 1024.0
epsilon = 1e-05

f32 = jnp.float32
VMEM_LIMIT = 56 * 1024 * 1024
LANES = 128

TOK_X = [(i, i ^ 1) for i in range(4)]
TOK_Y = [(i, i ^ 2) for i in range(4)]
TOK_D = [(i, i ^ 3) for i in range(4)]
SWAP = [(0, 1), (1, 0)]


def pow2(k):
    one = jnp.ones_like(k)
    a = jnp.left_shift(one, jnp.clip(k + 60, 0, 30)).astype(f32)
    b = jnp.left_shift(one, jnp.clip(k + 30, 0, 30)).astype(f32)
    c = jnp.left_shift(one, jnp.clip(k, 0, 30)).astype(f32)
    d = jnp.left_shift(one, jnp.clip(k - 30, 0, 30)).astype(f32)
    return (a * (2.0**-60)) * b * c * d


def encode(x):
    top = jnp.max(jnp.abs(x), axis=1, keepdims=True)
    e = jnp.ceil(jnp.log2(jnp.maximum(top, 2.0**-44))).astype(jnp.int32)
    e = jnp.clip(e, -44, 31)
    q = jnp.clip(jnp.round(x * pow2(15 - e)), -32767.0, 32767.0)
    return q.astype(jnp.int32).astype(jnp.int16), e


def decode(q, e):
    return q.astype(jnp.int32).astype(f32) * pow2(e - 15)


def lane_is(shape, j):
    return lax.broadcasted_iota(jnp.int32, shape, 1) == j


def logits_kernel(keep_q, send_q, quarter, tile, a_ref, h_ref, keep_ref, send_ref, exps):
    j = pl.program_id(0)
    r = lax.dot_general(
        a_ref[...], h_ref[...], (((1,), (1,)), ((), ())), preferred_element_type=f32
    )

    @pl.when(j == 0)
    def _():
        exps[...] = jnp.zeros_like(exps)

    for n, k in enumerate(keep_q):
        keep_ref[n * quarter : (n + 1) * quarter, :] = r[k * quarter : (k + 1) * quarter]
    columns = pl.ds(pl.multiple_of(j * tile, tile), tile)
    for n, k in enumerate(send_q):
        rows = slice(n * quarter, (n + 1) * quarter)
        q, e = encode(r[k * quarter : (k + 1) * quarter])
        send_ref[rows, columns] = q
        exps[rows, :] = jnp.where(lane_is((quarter, LANES), j), e, exps[rows, :])

    @pl.when(j == pl.num_programs(0) - 1)
    def _():
        send_ref[:, send_ref.shape[1] - LANES :] = exps[...].astype(jnp.int16)


def partial_logits(a, head, second, tile):
    rows, width = a.shape
    quarter = rows // 4
    half = head.shape[0] // 2
    tiles = half // tile
    first = tiles if second else 0
    keep_q, send_q = ((0, 1), (2, 3)) if second else ((0, 2), (1, 3))
    return pl.pallas_call(
        functools.partial(logits_kernel, keep_q, send_q, quarter, tile),
        grid=(tiles,),
        in_specs=[
            pl.BlockSpec((rows, width), lambda j: (0, 0)),
            pl.BlockSpec((tile, width), lambda j: (first + j, 0)),
        ],
        out_specs=[
            pl.BlockSpec((2 * quarter, tile), lambda j: (0, j)),
            pl.BlockSpec((2 * quarter, half + LANES), lambda j: (0, 0)),
        ],
        out_shape=[
            jax.ShapeDtypeStruct((2 * quarter, half), f32),
            jax.ShapeDtypeStruct((2 * quarter, half + LANES), jnp.int16),
        ],
        scratch_shapes=[pltpu.VMEM((2 * quarter, LANES), jnp.int32)],
        compiler_params=pltpu.CompilerParams(vmem_limit_bytes=VMEM_LIMIT),
        cost_estimate=pl.CostEstimate(
            flops=2 * rows * half * width,
            bytes_accessed=2 * half * width + 2 * rows * width + 6 * rows * half,
            transcendentals=0,
        ),
        name="logits",
    )(a, head)


def relay_kernel(tile, got_ref, keep_ref, out_ref):
    rows, half = keep_ref.shape
    exps = got_ref[:, half : half + LANES].astype(jnp.int32)
    new = jnp.zeros((rows, LANES), jnp.int32)
    for j in range(half // tile):
        cols = slice(j * tile, (j + 1) * tile)
        total = keep_ref[:, cols] + decode(got_ref[:, cols], exps[:, j : j + 1])
        q, e = encode(total)
        out_ref[:, cols] = q
        new = jnp.where(lane_is(new.shape, j), e, new)
    out_ref[:, half : half + LANES] = new.astype(jnp.int16)


def relay(got, keep, tile):
    quarter, half = keep.shape[0] // 2, keep.shape[1]
    return pl.pallas_call(
        functools.partial(relay_kernel, tile),
        grid=(1,),
        in_specs=[
            pl.BlockSpec((quarter, half + LANES), lambda j: (1, 0)),
            pl.BlockSpec((quarter, half), lambda j: (1, 0)),
        ],
        out_specs=pl.BlockSpec((quarter, half + LANES), lambda j: (0, 0)),
        out_shape=jax.ShapeDtypeStruct((quarter, half + LANES), jnp.int16),
        compiler_params=pltpu.CompilerParams(vmem_limit_bytes=VMEM_LIMIT),
        cost_estimate=pl.CostEstimate(
            flops=10 * quarter * half, bytes_accessed=8 * quarter * half, transcendentals=0
        ),
        name="relay",
    )(got, keep)


def put(stats, j, value):
    return jnp.where(lane_is(stats.shape, j), value, stats)


def summed(tile, half, keeps, gots, lasts, inv, out_ref):
    top = None
    for p in range(2):
        first = gots[p][:, half : half + LANES].astype(jnp.int32)
        last = lasts[p][:, half : half + LANES].astype(jnp.int32)
        for j in range(half // tile):
            cols = slice(j * tile, (j + 1) * tile)
            x = keeps[p][:, cols] + decode(gots[p][:, cols], first[:, j : j + 1])
            x = (x + decode(lasts[p][:, cols], last[:, j : j + 1])) * inv
            out_ref[:, p * half + j * tile : p * half + (j + 1) * tile] = x
            high = jnp.max(x, axis=1, keepdims=True)
            top = high if top is None else jnp.maximum(top, high)
    return top


def student_kernel(
    tile, base_ref, kp, kq, gp, gq, lp, lq, inv_ref, target_ref, out_ref, stats_ref
):
    rows, half = kp.shape
    top = summed(tile, half, (kp, kq), (gp, gq), (lp, lq), inv_ref[...], out_ref)
    soft = jnp.zeros((rows, 1), f32)
    plain = jnp.zeros((rows, 1), f32)
    hit = jnp.zeros((rows, 1), f32)
    target = target_ref[...] - base_ref[0]
    for j in range(2 * half // tile):
        x = out_ref[:, j * tile : (j + 1) * tile]
        warm = jnp.exp((x - top) * (1.0 / heat))
        soft = soft + jnp.sum(warm, axis=1, keepdims=True)
        plain = plain + jnp.sum(warm * warm, axis=1, keepdims=True)
        here = lane_is(x.shape, target - j * tile)
        hit = hit + jnp.sum(jnp.where(here, x, 0.0), axis=1, keepdims=True)
    stats = jnp.zeros((rows, LANES), f32)
    for n, value in enumerate((top, soft, plain, hit)):
        stats = put(stats, n, value)
    stats_ref[...] = stats


def teacher_kernel(
    tile, kp, kq, gp, gq, lp, lq, inv_ref, student_ref, before_ref, out_ref, stats_ref
):
    rows, half = kp.shape
    top = summed(tile, half, (kp, kq), (gp, gq), (lp, lq), inv_ref[...], out_ref)
    top = top * (1.0 / heat)
    total = jnp.zeros((rows, 1), f32)
    cross = jnp.zeros((rows, 1), f32)
    for j in range(2 * half // tile):
        cols = slice(j * tile, (j + 1) * tile)
        x = out_ref[:, cols]
        power = jnp.exp(x * (1.0 / heat) - top)
        total = total + jnp.sum(power, axis=1, keepdims=True)
        gap = (x - student_ref[:, cols]) * (1.0 / heat)
        cross = cross + jnp.sum(power * gap, axis=1, keepdims=True)
    stats = before_ref[...]
    for n, value in enumerate((top, total, cross)):
        stats = put(stats, 4 + n, value)
    stats_ref[...] = stats


def finish(keeps, gots, lasts, inv, extra, tile):
    quarter, half = keeps[0].shape[0] // 2, keeps[0].shape[1]
    wide = pl.BlockSpec((quarter, half + LANES), lambda j: (0, 0))
    column = pl.BlockSpec((quarter, 1), lambda j: (0, 0))
    whole = pl.BlockSpec((quarter, 2 * half), lambda j: (0, 0))
    stat = pl.BlockSpec((quarter, LANES), lambda j: (0, 0))
    operands = (*keeps, *gots, *lasts, inv)
    specs = [pl.BlockSpec((quarter, half), lambda j: (0, 0))] * 2 + [wide] * 4 + [column]
    if extra[0].shape == (1,):
        body = student_kernel
        operands = (extra[0], *operands, extra[1])
        specs = [pl.BlockSpec(memory_space=pltpu.SMEM)] + specs + [column]
    else:
        body = teacher_kernel
        operands = (*operands, *extra)
        specs = specs + [whole, stat]
    return pl.pallas_call(
        functools.partial(body, tile),
        grid=(1,),
        in_specs=specs,
        out_specs=[whole, stat],
        out_shape=[
            jax.ShapeDtypeStruct((quarter, 2 * half), f32),
            jax.ShapeDtypeStruct((quarter, LANES), f32),
        ],
        compiler_params=pltpu.CompilerParams(vmem_limit_bytes=VMEM_LIMIT),
        cost_estimate=pl.CostEstimate(
            flops=30 * quarter * half, bytes_accessed=24 * quarter * half, transcendentals=0
        ),
        name="finish",
    )(*operands)


def tree_sum(parts):
    while len(parts) > 1:
        parts = [a + b for a, b in zip(parts[::2], parts[1::2])]
    return parts[0]


def slope_kernel(
    tile, base_ref, student_ref, teacher_ref, stats_ref, target_ref, grad_ref, loss_ref
):
    rows, width = student_ref.shape
    sets = stats_ref.shape[0]
    all_stats = [stats_ref[k] for k in range(sets)]
    top = functools.reduce(jnp.maximum, all_stats)

    def scaled(lane, top_lane, rate):
        return tree_sum(
            [
                s[:, lane : lane + 1]
                * jnp.exp((s[:, top_lane : top_lane + 1] - top[:, top_lane : top_lane + 1]) * rate)
                for s in all_stats
            ]
        )

    student_top, teacher_top = top[:, 0:1], top[:, 4:5]
    soft_total = scaled(1, 0, 1.0 / heat)
    plain_total = scaled(2, 0, 1.0)
    teacher_total = scaled(5, 4, 1.0)
    cross_total = scaled(6, 4, 1.0)
    label = tree_sum([s[:, 3:4] for s in all_stats])
    row_loss = blend * heat**2 * (
        cross_total / teacher_total
        - teacher_top
        - jnp.log(teacher_total)
        + student_top / heat
        + jnp.log(soft_total)
    ) + (1.0 - blend) * (student_top + jnp.log(plain_total) - label)
    loss_ref[...] = put(jnp.zeros((rows, LANES), f32), 0, row_loss)

    soft_rate = grad_scale * blend * heat / soft_total
    teacher_rate = grad_scale * blend * heat / teacher_total
    plain_rate = grad_scale * (1.0 - blend) / plain_total
    target = target_ref[...] - base_ref[0]
    for j in range(width // tile):
        cols = slice(j * tile, (j + 1) * tile)
        warm = jnp.exp((student_ref[:, cols] - student_top) * (1.0 / heat))
        power = jnp.exp(teacher_ref[:, cols] * (1.0 / heat) - teacher_top)
        g = warm * (soft_rate + plain_rate * warm) - power * teacher_rate
        here = lane_is(g.shape, target - j * tile)
        g = jnp.where(here, g - grad_scale * (1.0 - blend), g)
        grad_ref[:, cols] = g.astype(jnp.bfloat16)


def slope(base, student, teacher, stats, targets, tile):
    rows, width = student.shape
    vmem = pl.BlockSpec(memory_space=pltpu.VMEM)
    return pl.pallas_call(
        functools.partial(slope_kernel, tile),
        in_specs=[pl.BlockSpec(memory_space=pltpu.SMEM)] + [vmem] * 4,
        out_specs=[vmem] * 2,
        out_shape=[
            jax.ShapeDtypeStruct((rows, width), jnp.bfloat16),
            jax.ShapeDtypeStruct((rows, LANES), f32),
        ],
        compiler_params=pltpu.CompilerParams(vmem_limit_bytes=VMEM_LIMIT),
        cost_estimate=pl.CostEstimate(
            flops=20 * rows * width, bytes_accessed=10 * rows * width, transcendentals=0
        ),
        name="slope",
    )(base, student, teacher, stats, targets)


def norm_grad_kernel(quarter, half, t_ref, own, gx, gy, dp, dq, h_ref, out_ref, lhs):
    @pl.when(pl.program_id(0) == 0)
    def _():
        for n, ref in enumerate((own, gx, gy)):
            lhs[n * quarter : (n + 1) * quarter, :] = ref[...]
        lhs[3 * quarter :, :half] = dp[...]
        lhs[3 * quarter :, half:] = dq[...]

    r = jnp.dot(lhs[...], h_ref[...], preferred_element_type=f32)
    t = t_ref[0]
    for n in range(4):
        place = pl.multiple_of(jnp.bitwise_xor(t, n) * quarter, quarter)
        out_ref[pl.ds(place, quarter), :] = r[n * quarter : (n + 1) * quarter]


def norm_gradient(t, own, gx, gy, dp, dq, head):
    quarter, vocab = own.shape
    width = head.shape[1]
    tile = min(256, width)
    half = vocab // 2
    full = pl.BlockSpec((quarter, vocab), lambda j: (0, 0))
    part = pl.BlockSpec((quarter, half), lambda j: (0, 0))
    return pl.pallas_call(
        functools.partial(norm_grad_kernel, quarter, half),
        grid=(width // tile,),
        in_specs=[
            pl.BlockSpec(memory_space=pltpu.SMEM),
            full,
            full,
            full,
            part,
            part,
            pl.BlockSpec((vocab, tile), lambda j: (0, j)),
        ],
        out_specs=pl.BlockSpec((4 * quarter, tile), lambda j: (0, j)),
        out_shape=jax.ShapeDtypeStruct((4 * quarter, width), f32),
        scratch_shapes=[pltpu.VMEM((4 * quarter, vocab), jnp.bfloat16)],
        compiler_params=pltpu.CompilerParams(vmem_limit_bytes=VMEM_LIMIT),
        cost_estimate=pl.CostEstimate(
            flops=8 * quarter * vocab * width,
            bytes_accessed=2 * vocab * width + 8 * quarter * vocab,
            transcendentals=0,
        ),
        name="norm_grad",
    )(t, own, gx, gy, dp, dq, head)


def tok_sum(x):
    a = lax.ppermute(x, "tok", TOK_X)
    b = lax.ppermute(x, "tok", TOK_Y)
    c = lax.ppermute(x, "tok", TOK_D)
    return (x + a) + (b + c)


def range_gather(x):
    grps, vocabs = lax.axis_size("grp"), lax.axis_size("vocab")
    me = lax.axis_index(("grp", "vocab"))
    if grps == 2 and vocabs == 4:
        pair = jnp.stack([x, lax.ppermute(x, "grp", SWAP)])
        sets = [pair]
        for k in range(1, 4):
            sets.append(lax.ppermute(pair, "vocab", [(i, i ^ k) for i in range(4)]))
        place = jnp.array([(k % 2) * 4 + k // 2 for k in range(8)], jnp.int32)
        return jnp.concatenate(sets), jnp.bitwise_xor(me, place)
    return lax.all_gather(x, ("grp", "vocab"), axis=0), jnp.arange(grps * vocabs)


def on_device(
    teacher_hidden,
    student_hidden,
    teacher_gain,
    student_gain,
    teacher_head,
    student_head,
    target_ids,
):
    blocks = lax.axis_size("grp") * lax.axis_size("vocab")
    own_rows = teacher_hidden.shape[0]
    all_rows = blocks * own_rows
    part_rows = own_rows // 2
    quarter = blocks * part_rows // 4
    vocab_local = teacher_head.shape[0]
    half = vocab_local // 2
    tile = min(512, half)
    teacher_width = teacher_hidden.shape[1] * lax.axis_size("tok")
    student_width = student_hidden.shape[1] * lax.axis_size("tok")
    t = lax.axis_index("tok")
    t_arr = t.astype(jnp.int32).reshape(1)
    base = (lax.axis_index(("grp", "vocab")) * vocab_local).astype(jnp.int32).reshape(1)

    halves = [slice(0, part_rows), slice(part_rows, own_rows)]
    gathered = []
    for rows in halves:
        s = lax.all_gather(student_hidden[rows], ("grp", "vocab"), axis=0, tiled=True)
        h = lax.all_gather(teacher_hidden[rows], ("grp", "vocab"), axis=0, tiled=True)
        gathered.append((s, h))

    student_wide = student_hidden.astype(f32)
    teacher_wide = teacher_hidden.astype(f32)
    squares = jnp.stack(
        [jnp.sum(student_wide * student_wide, axis=1), jnp.sum(teacher_wide * teacher_wide, axis=1)]
    )
    squares = tok_sum(squares)
    widths = jnp.array([[student_width], [teacher_width]], f32)
    inverse = lax.rsqrt(squares / widths + epsilon)
    everyone, order = range_gather(inverse)
    everyone = jnp.zeros_like(everyone).at[order].set(everyone)
    targets = target_ids.reshape(blocks, own_rows)

    def weighted(rows, gain):
        q = rows.reshape(4, quarter, rows.shape[1])
        q = jnp.concatenate(
            [lax.dynamic_slice_in_dim(q, jnp.bitwise_xor(t, k), 1, 0) for k in range(4)]
        )
        return (q.astype(f32) * gain).astype(jnp.bfloat16).reshape(rows.shape)

    def mine(x, part):
        x = x[:, halves[part]].reshape(4 * quarter)
        return lax.dynamic_slice_in_dim(x, t * quarter, quarter).reshape(quarter, 1)

    def logits_sum(a, head):
        keep_p, send_p = partial_logits(a, head, False, tile)
        keep_q, send_q = partial_logits(a, head, True, tile)
        got_p = lax.ppermute(send_p, "tok", TOK_X)
        got_q = lax.ppermute(send_q, "tok", TOK_Y)
        last_p = lax.ppermute(relay(got_p, keep_p, tile), "tok", TOK_Y)
        last_q = lax.ppermute(relay(got_q, keep_q, tile), "tok", TOK_X)
        return (keep_p, keep_q), (got_p, got_q), (last_p, last_q)

    losses = 0.0
    outs = []
    for part in range(2):
        rows_s, rows_t = gathered[part]
        row_targets = mine(targets, part)
        student_sums = logits_sum(weighted(rows_s, student_gain), student_head)
        teacher_sums = logits_sum(weighted(rows_t, teacher_gain), teacher_head)
        student_logits, stats = finish(
            *student_sums, mine(everyone[:, 0], part), (base, row_targets), tile
        )
        teacher_logits, stats = finish(
            *teacher_sums, mine(everyone[:, 1], part), (student_logits, stats), tile
        )
        all_stats, _ = range_gather(stats)
        grad, row_loss = slope(base, student_logits, teacher_logits, all_stats, row_targets, tile)
        losses = losses + jnp.sum(row_loss[:, 0])
        gx = lax.ppermute(grad, "tok", TOK_X)
        gy = lax.ppermute(grad, "tok", TOK_Y)
        dp = lax.ppermute(gx[:, :half], "tok", TOK_Y)
        dq = lax.ppermute(gy[:, half:], "tok", TOK_X)
        outs.append(norm_gradient(t_arr, grad, gx, gy, dp, dq, student_head))

    norm_grad = jnp.concatenate(
        [
            lax.psum_scatter(o, ("grp", "vocab"), scatter_dimension=0, tiled=True)
            for o in outs
        ]
    )
    inner_local = jnp.sum(student_gain * norm_grad * student_wide, axis=1)
    last = tok_sum(jnp.concatenate([inner_local, jnp.reshape(losses, (1,))]))
    loss = last[own_rows] / all_rows
    inner = last[:own_rows]
    own_inv = inverse[0]
    hidden_grad = (
        own_inv[:, None] * student_gain * norm_grad
        - student_wide * (own_inv**3 * inner / student_width)[:, None]
    ).astype(jnp.bfloat16)
    return (loss, hidden_grad)


def solution(mesh):
    in_specs = (
        P(("grp", "vocab"), "tok"),
        P(("grp", "vocab"), "tok"),
        P("tok"),
        P("tok"),
        P(("grp", "vocab"), "tok"),
        P(("grp", "vocab"), "tok"),
        P(),
    )
    out_specs = (P(), P(("grp", "vocab"), "tok"))
    return jax.shard_map(
        on_device, mesh=mesh, in_specs=in_specs, out_specs=out_specs, check_vma=False
    )
```

```python
import functools
import jax
import jax.numpy as jnp
from jax import lax
from jax.experimental import pallas as pl
from jax.experimental.pallas import tpu as pltpu
from jax.sharding import PartitionSpec as P

heat = 2.0
blend = 0.5
grad_scale = 1024.0
epsilon = 1e-05

f32 = jnp.float32
VMEM_LIMIT = 56 * 1024 * 1024
LANES = 128
QUARTER = LANES // 2
PAD = 16
BLOCK_BYTES = 8 * 1024 * 1024

TOK_X = [(i, i ^ 1) for i in range(4)]
TOK_Y = [(i, i ^ 2) for i in range(4)]
TOK_D = [(i, i ^ 3) for i in range(4)]
SWAP = [(0, 1), (1, 0)]

VMEM = pl.BlockSpec(memory_space=pltpu.VMEM)
SMEM = pl.BlockSpec(memory_space=pltpu.SMEM)
ANY = pl.BlockSpec(memory_space=pl.ANY)
PARAMS = pltpu.CompilerParams(vmem_limit_bytes=VMEM_LIMIT)


LIGHT = pl.CostEstimate(flops=1024, bytes_accessed=1024, transcendentals=0)


def pow2(k):
    one = jnp.ones_like(k)
    a = jnp.left_shift(one, jnp.clip(k + 60, 0, 30)).astype(f32)
    b = jnp.left_shift(one, jnp.clip(k + 30, 0, 30)).astype(f32)
    c = jnp.left_shift(one, jnp.clip(k, 0, 30)).astype(f32)
    d = jnp.left_shift(one, jnp.clip(k - 30, 0, 30)).astype(f32)
    return (a * (2.0**-60)) * b * c * d


def encode(x):
    top = jnp.max(jnp.abs(x), axis=0, keepdims=True)
    e = jnp.ceil(jnp.log2(jnp.maximum(top, 2.0**-44))).astype(jnp.int32)
    e = jnp.clip(e, -44, 31)
    q = jnp.clip(jnp.round(x * pow2(15 - e)), -32767.0, 32767.0)
    return q.astype(jnp.int32).astype(jnp.int16), e


def decode(q, e):
    return q.astype(jnp.int32).astype(f32) * pow2(e - 15)


def low_lanes(shape):
    return lax.broadcasted_iota(jnp.int32, shape, 1) < QUARTER


def swap_lanes(x):
    return pltpu.roll(x, QUARTER, 1)


def row_is(shape, j):
    return lax.broadcasted_iota(jnp.int32, shape, 0) == j


ORDER = ((0, 2, 1, 3), (0, 1, 2, 3))


def logits_kernel(parts, tiles, tile, t_ref, rows_ref, gain_ref, h_ref, dep_ref, *refs):
    outs, (a_ref, exps) = refs[: 2 * len(parts)], refs[2 * len(parts) :]
    j = pl.program_id(0)

    @pl.when(j == 0)
    def _():
        t = t_ref[0]
        for k in range(4):
            place = pl.multiple_of(jnp.bitwise_xor(t, k) * QUARTER, QUARTER)
            w = rows_ref[pl.ds(place, QUARTER), :].astype(f32) * gain_ref[...]
            w = w.astype(jnp.bfloat16)
            for n, part in enumerate(parts):
                at = ORDER[part].index(k) * QUARTER
                a_ref[n, at : at + QUARTER, :] = w

    for n in range(len(parts)):
        keep_ref, send_ref = outs[2 * n], outs[2 * n + 1]
        half = send_ref.shape[0] - PAD

        @pl.when((j >= n * tiles) & (j < (n + 1) * tiles))
        def _():
            r = lax.dot_general(
                h_ref[...], a_ref[n], (((1,), (1,)), ((), ())), preferred_element_type=f32
            )
            keep_ref[...] = r[:, :LANES]
            q, e = encode(r[:, LANES:])
            at = j - n * tiles
            send_ref[pl.ds(pl.multiple_of(at * tile, tile), tile), :] = q
            before = jnp.where(at == 0, 0, exps[...])
            exps[...] = jnp.where(row_is((PAD, LANES), at), e, before)

            @pl.when(at == tiles - 1)
            def _():
                send_ref[half:, :] = exps[...].astype(jnp.int16)


def logits_tile(head):
    return min(BLOCK_BYTES // (2 * head.shape[1]), head.shape[0] // 2)


def partial_logits(t, rows, gain, head, parts, dep):
    count, width = rows.shape[0], head.shape[1]
    half = head.shape[0] // 2
    tile = logits_tile(head)
    tiles = half // tile
    first = parts[0] * tiles
    out_specs, out_shape = [], []
    for n in range(len(parts)):
        out_specs += [
            pl.BlockSpec(
                (tile, LANES), lambda j, n=n: (jnp.clip(j - n * tiles, 0, tiles - 1), 0)
            ),
            pl.BlockSpec((half + PAD, LANES), lambda j: (0, 0)),
        ]
        out_shape += [
            jax.ShapeDtypeStruct((half, LANES), f32),
            jax.ShapeDtypeStruct((half + PAD, LANES), jnp.int16),
        ]
    return pl.pallas_call(
        functools.partial(logits_kernel, parts, tiles, tile),
        grid=(len(parts) * tiles,),
        in_specs=[
            SMEM,
            pl.BlockSpec((count, width), lambda j: (0, 0)),
            pl.BlockSpec((1, width), lambda j: (0, 0)),
            pl.BlockSpec((tile, width), lambda j: (first + j, 0)),
            ANY,
        ],
        out_specs=out_specs,
        out_shape=out_shape,
        scratch_shapes=[
            pltpu.VMEM((len(parts), count, width), jnp.bfloat16),
            pltpu.VMEM((PAD, LANES), jnp.int32),
        ],
        compiler_params=PARAMS,
        cost_estimate=LIGHT,
        name="logits",
    )(t, rows, gain.reshape(1, width), head, dep)


def relay_kernel(step, tile, *refs):
    ins, outs, news = refs[:11], refs[11:15], refs[15:]
    n, steps = pl.program_id(0), pl.num_programs(0)
    for p in range(2):
        got_top, got_low, exps_ref, keep_top, keep_low = ins[5 * p : 5 * p + 5]
        next_ref, own_ref, new = outs[2 * p], outs[2 * p + 1], news[p]
        exps = exps_ref[...].astype(jnp.int32)

        def exponent(at):
            here = row_is(exps.shape, at // tile)
            return jnp.sum(jnp.where(here, exps, 0), axis=0, keepdims=True)

        top = keep_top[...] + decode(got_top[...], exponent(n * step))
        low = keep_low[...] + decode(got_low[...], exponent((steps + n) * step))
        mask = low_lanes(top.shape)
        own_ref[...] = jnp.where(mask, top, swap_lanes(low))
        q, e = encode(jnp.where(mask, swap_lanes(top), low))
        next_ref[pl.ds(pl.multiple_of(n * step, step), step), :] = q
        before = jnp.where(n == 0, 0, new[...])
        new[...] = jnp.where(row_is(new.shape, n), e, before)

        @pl.when(n == steps - 1)
        def _():
            next_ref[steps * step :, :] = new[...].astype(jnp.int16)


def relay(gots, keeps, tile, dep):
    half = keeps[0].shape[0]
    step = min(512, half // 2)
    steps = half // 2 // step
    top = pl.BlockSpec((step, LANES), lambda n: (n, 0))
    low = pl.BlockSpec((step, LANES), lambda n: (steps + n, 0))
    exps = pl.BlockSpec((PAD, LANES), lambda n: (half // PAD, 0))
    shapes = [
        jax.ShapeDtypeStruct((half // 2 + PAD, LANES), jnp.int16),
        jax.ShapeDtypeStruct((half // 2, LANES), f32),
    ]
    operands = []
    for got, keep in zip(gots, keeps):
        operands += [got, got, got, keep, keep]
    return pl.pallas_call(
        functools.partial(relay_kernel, step, tile),
        grid=(steps,),
        in_specs=[top, low, exps, top, low] * 2 + [ANY],
        out_specs=[pl.BlockSpec((half // 2 + PAD, LANES), lambda n: (0, 0)), top] * 2,
        out_shape=shapes * 2,
        scratch_shapes=[pltpu.VMEM((PAD, LANES), jnp.int32)] * 2,
        compiler_params=PARAMS,
        cost_estimate=LIGHT,
        name="relay",
    )(*operands, dep)


def merged(op, x):
    return op(x, swap_lanes(x))


def summed(owns, lasts, inv, out_ref):
    top = None
    for p in range(2):
        packed = owns[p].shape[0]
        step = min(512, packed)
        exps = lasts[p][packed : packed + PAD, :].astype(jnp.int32)
        for n in range(packed // step):
            rows = slice(n * step, (n + 1) * step)
            x = owns[p][rows, :] + decode(lasts[p][rows, :], exps[n : n + 1, :])
            x = x * inv
            out_ref[p * packed + n * step : p * packed + (n + 1) * step, :] = x
            high = jnp.max(x, axis=0, keepdims=True)
            top = high if top is None else jnp.maximum(top, high)
    return merged(jnp.maximum, top)


def places(shape, at, packed):
    part, start = at // packed, at % packed
    row = lax.broadcasted_iota(jnp.int32, shape, 0) + (2 * part * packed + start)
    return jnp.where(low_lanes(shape), row, row + packed)


def student_kernel(op, oq, lp, lq, inv_ref, target_ref, base_ref, dep, out_ref, stats_ref):
    packed = op.shape[0]
    step = min(512, packed)
    top = summed((op, oq), (lp, lq), inv_ref[...], out_ref)
    soft = jnp.zeros((1, LANES), f32)
    plain = jnp.zeros((1, LANES), f32)
    hit = jnp.zeros((1, LANES), f32)
    target = target_ref[...] - base_ref[0]
    for n in range(2 * packed // step):
        x = out_ref[n * step : (n + 1) * step, :]
        warm = jnp.exp((x - top) * (1.0 / heat))
        soft = soft + jnp.sum(warm, axis=0, keepdims=True)
        plain = plain + jnp.sum(warm * warm, axis=0, keepdims=True)
        here = places(x.shape, n * step, packed) == target
        hit = hit + jnp.sum(jnp.where(here, x, 0.0), axis=0, keepdims=True)
    stats = jnp.zeros((8, LANES), f32)
    sums = [merged(jnp.add, v) for v in (soft, plain, hit)]
    for n, value in enumerate([top] + sums):
        stats = jnp.where(row_is(stats.shape, n), value, stats)
    stats_ref[...] = stats


def teacher_kernel(op, oq, lp, lq, inv_ref, student_ref, before_ref, dep, out_ref, stats_ref):
    packed = op.shape[0]
    step = min(512, packed)
    top = summed((op, oq), (lp, lq), inv_ref[...], out_ref)
    top = top * (1.0 / heat)
    total = jnp.zeros((1, LANES), f32)
    cross = jnp.zeros((1, LANES), f32)
    for n in range(2 * packed // step):
        rows = slice(n * step, (n + 1) * step)
        x = out_ref[rows, :]
        power = jnp.exp(x * (1.0 / heat) - top)
        total = total + jnp.sum(power, axis=0, keepdims=True)
        gap = (x - student_ref[rows, :]) * (1.0 / heat)
        cross = cross + jnp.sum(power * gap, axis=0, keepdims=True)
    stats = before_ref[...]
    sums = [merged(jnp.add, v) for v in (total, cross)]
    for n, value in enumerate([top] + sums):
        stats = jnp.where(row_is(stats.shape, 4 + n), value, stats)
    stats_ref[...] = stats


def finish(body, owns, lasts, inv, extra, dep):
    packed = owns[0].shape[0]
    last_spec = SMEM if body is student_kernel else VMEM
    return pl.pallas_call(
        body,
        in_specs=[VMEM] * 6 + [last_spec, ANY],
        out_specs=[VMEM] * 2,
        out_shape=[
            jax.ShapeDtypeStruct((2 * packed, LANES), f32),
            jax.ShapeDtypeStruct((8, LANES), f32),
        ],
        compiler_params=PARAMS,
        cost_estimate=LIGHT,
        name="finish",
    )(*owns, *lasts, inv, *extra, dep)


def tree_sum(parts):
    while len(parts) > 1:
        parts = [a + b for a, b in zip(parts[::2], parts[1::2])]
    return parts[0]


def slope_kernel(
    student_ref, teacher_ref, stats_ref, target_ref, base_ref, dep, grad_ref, loss_ref
):
    packed = student_ref.shape[0] // 2
    step = min(512, packed)
    sets = [stats_ref[k] for k in range(stats_ref.shape[0])]
    top = functools.reduce(jnp.maximum, sets)

    def scaled(row, top_row, rate):
        high = top[top_row : top_row + 1]
        return tree_sum(
            [s[row : row + 1] * jnp.exp((s[top_row : top_row + 1] - high) * rate) for s in sets]
        )

    student_top, teacher_top = top[0:1], top[4:5]
    soft_total = scaled(1, 0, 1.0 / heat)
    plain_total = scaled(2, 0, 1.0)
    teacher_total = scaled(5, 4, 1.0)
    cross_total = scaled(6, 4, 1.0)
    label = tree_sum([s[3:4] for s in sets])
    row_loss = blend * heat**2 * (
        cross_total / teacher_total
        - teacher_top
        - jnp.log(teacher_total)
        + student_top / heat
        + jnp.log(soft_total)
    ) + (1.0 - blend) * (student_top + jnp.log(plain_total) - label)
    soft_rate = grad_scale * blend * heat / soft_total
    teacher_rate = grad_scale * blend * heat / teacher_total
    plain_rate = grad_scale * (1.0 - blend) / plain_total
    inner = jnp.zeros((1, LANES), f32)
    target = target_ref[...] - base_ref[0]
    for n in range(2 * packed // step):
        rows = slice(n * step, (n + 1) * step)
        logits = student_ref[rows, :]
        warm = jnp.exp((logits - student_top) * (1.0 / heat))
        power = jnp.exp(teacher_ref[rows, :] * (1.0 / heat) - teacher_top)
        g = warm * (soft_rate + plain_rate * warm) - power * teacher_rate
        here = places(g.shape, n * step, packed) == target
        g = jnp.where(here, g - grad_scale * (1.0 - blend), g)
        g = g.astype(jnp.bfloat16).astype(f32)
        inner = inner + jnp.sum(g * logits, axis=0, keepdims=True)
        g = jnp.transpose(g).astype(jnp.bfloat16)
        at = 2 * (n * step // packed) * packed + (n * step) % packed
        grad_ref[:, at : at + step] = g[:QUARTER]
        grad_ref[:, at + packed : at + packed + step] = g[QUARTER:]
    rows_out = jnp.where(row_is((8, LANES), 0), row_loss, 0.0)
    loss_ref[...] = jnp.where(row_is((8, LANES), 1), merged(jnp.add, inner), rows_out)


def slope(base, student, teacher, stats, targets, dep):
    return pl.pallas_call(
        slope_kernel,
        in_specs=[VMEM] * 4 + [SMEM, ANY],
        out_specs=[VMEM] * 2,
        out_shape=[
            jax.ShapeDtypeStruct((QUARTER, 2 * student.shape[0]), jnp.bfloat16),
            jax.ShapeDtypeStruct((8, LANES), f32),
        ],
        compiler_params=PARAMS,
        cost_estimate=LIGHT,
        name="slope",
    )(student, teacher, stats, targets, base, dep)


def norm_grad_kernel(t_ref, flip_ref, own, gx, gy, dp, dq, h_ref, dep, keep_ref, send_ref, lhs):
    half = dp.shape[1]

    @pl.when(pl.program_id(0) == 0)
    def _():
        for n, ref in enumerate((own, gx, gy)):
            lhs[n * QUARTER : (n + 1) * QUARTER, :] = ref[...]
        lhs[3 * QUARTER :, :half] = dp[...]
        lhs[3 * QUARTER :, half:] = dq[...]

    r = jnp.dot(lhs[...], h_ref[...], preferred_element_type=f32)
    t = jnp.bitwise_xor(t_ref[0], 2 * flip_ref[0])
    for n in range(4):
        quarter = jnp.bitwise_xor(t, n)
        at = pl.ds(pl.multiple_of(lax.rem(quarter, 2) * QUARTER, QUARTER), QUARTER)

        @pl.when(quarter < 2)
        def _():
            keep_ref[at, :] = r[n * QUARTER : (n + 1) * QUARTER]

        @pl.when(quarter >= 2)
        def _():
            send_ref[at, :] = r[n * QUARTER : (n + 1) * QUARTER]


def norm_gradient(t, flip, own, gx, gy, dp, dq, head, dep):
    vocab, width = head.shape
    tile = min(512, width)
    full = pl.BlockSpec((QUARTER, vocab), lambda j: (0, 0))
    part = pl.BlockSpec((QUARTER, vocab // 2), lambda j: (0, 0))
    return pl.pallas_call(
        norm_grad_kernel,
        grid=(width // tile,),
        in_specs=[SMEM, SMEM, full, full, full, part, part]
        + [pl.BlockSpec((vocab, tile), lambda j: (0, j)), ANY],
        out_specs=[pl.BlockSpec((2 * QUARTER, tile), lambda j: (0, j))] * 2,
        out_shape=[jax.ShapeDtypeStruct((2 * QUARTER, width), f32)] * 2,
        scratch_shapes=[pltpu.VMEM((4 * QUARTER, vocab), jnp.bfloat16)],
        compiler_params=PARAMS,
        cost_estimate=LIGHT,
        name="norm_grad",
    )(t, flip, own, gx, gy, dp, dq, head, dep)


def row_encode(x):
    top = jnp.max(jnp.abs(x), axis=1, keepdims=True)
    e = jnp.ceil(jnp.log2(jnp.maximum(top, 2.0**-44))).astype(jnp.int32)
    e = jnp.clip(e, -44, 44)
    q = jnp.clip(jnp.round(x * pow2(15 - e)), -32767.0, 32767.0)
    return q.astype(jnp.int32).astype(jnp.int16), e


def fold_kernel(z_ref, mine_ref, other_ref, own_ref, *sends):
    rows, width = own_ref.shape
    for k in range(4):
        at = pl.ds(pl.multiple_of(jnp.bitwise_xor(z_ref[0], k) * rows, rows), rows)
        x = mine_ref[at, :] + other_ref[at, :]
        if k == 0:
            own_ref[...] = x
        else:
            q, e = row_encode(x)
            sends[k - 1][:, :width] = q
            sends[k - 1][:, width:] = jnp.broadcast_to(e, (rows, LANES)).astype(jnp.int16)


def fold(z, mine, other):
    rows, width = other.shape
    return pl.pallas_call(
        fold_kernel,
        grid=(1,),
        in_specs=[
            SMEM,
            pl.BlockSpec((rows, width), lambda j: (0, 0)),
            pl.BlockSpec((rows, width), lambda j: (0, 0)),
        ],
        out_specs=[VMEM] * 4,
        out_shape=[jax.ShapeDtypeStruct((rows // 4, width), f32)]
        + [jax.ShapeDtypeStruct((rows // 4, width + LANES), jnp.int16)] * 3,
        compiler_params=PARAMS,
        cost_estimate=LIGHT,
        name="fold",
    )(z, mine, other)


def last_kernel(own_ref, p1, p2, p3, hidden_ref, gain_ref, inv_ref, inner_ref, out_ref):
    width = own_ref.shape[1]
    norm = own_ref[...]
    for p in (p1, p2, p3):
        e = p[:, width:].astype(jnp.int32)[:, :1]
        norm = norm + p[:, :width].astype(jnp.int32).astype(f32) * pow2(e - 15)
    out = inv_ref[...] * gain_ref[...] * norm - hidden_ref[...].astype(f32) * inner_ref[...]
    out_ref[...] = out.astype(jnp.bfloat16)


def last(own, gots, hidden, gain, inv, inner):
    return pl.pallas_call(
        last_kernel,
        in_specs=[VMEM] * 8,
        out_specs=VMEM,
        out_shape=jax.ShapeDtypeStruct(own.shape, jnp.bfloat16),
        compiler_params=PARAMS,
        cost_estimate=LIGHT,
        name="hidden_grad",
    )(own, *gots, hidden, gain.reshape(1, -1), inv[:, None], inner[:, None])


def tok_sum(x):
    a = lax.ppermute(x, "tok", TOK_X)
    b = lax.ppermute(x, "tok", TOK_Y)
    c = lax.ppermute(x, "tok", TOK_D)
    return (x + a) + (b + c)


def small_box():
    return lax.axis_size("grp") == 2 and lax.axis_size("vocab") == 4


def along_z(x):
    return [x] + [lax.ppermute(x, "vocab", [(i, i ^ k) for i in range(4)]) for k in range(1, 4)]


def range_gather(x, ordered):
    if not small_box():
        return lax.all_gather(x, ("grp", "vocab"), axis=0)
    own = jnp.stack(along_z(x))
    sets = jnp.concatenate([own, lax.ppermute(own, "grp", SWAP)])
    if ordered:
        sets = sets[jnp.bitwise_xor(lax.axis_index(("grp", "vocab")), jnp.arange(8))]
    return sets


def on_device(
    teacher_hidden,
    student_hidden,
    teacher_gain,
    student_gain,
    teacher_head,
    student_head,
    target_ids,
):
    blocks = lax.axis_size("grp") * lax.axis_size("vocab")
    own_rows = teacher_hidden.shape[0]
    all_rows = blocks * own_rows
    part_rows = own_rows // 2
    vocab_local = teacher_head.shape[0]
    half = vocab_local // 2
    teacher_width = teacher_hidden.shape[1] * lax.axis_size("tok")
    student_width = student_hidden.shape[1] * lax.axis_size("tok")
    t = lax.axis_index("tok")
    t_arr = t.astype(jnp.int32).reshape(1)
    base = (lax.axis_index(("grp", "vocab")) * vocab_local).astype(jnp.int32).reshape(1)

    halves = [slice(0, part_rows), slice(part_rows, own_rows)]

    def gather_rows(x, after=None):
        if after is not None:
            x, _ = lax.optimization_barrier((x, after))
        return lax.all_gather(x, ("grp", "vocab"), axis=0, tiled=True)

    if small_box():
        near = along_z(student_hidden[halves[0]])
        sets = jnp.stack(near)
        sets = jnp.concatenate([sets, lax.ppermute(sets, "grp", SWAP)])
        place = jnp.bitwise_xor(lax.axis_index(("grp", "vocab")), jnp.arange(blocks))
        student_a = sets[place].reshape(blocks * part_rows, -1)
        first = near[1]
    else:
        student_a = gather_rows(student_hidden[halves[0]])
        first = student_a
    teacher_a = gather_rows(teacher_hidden[halves[0]], first)

    student_wide, teacher_wide, _ = lax.optimization_barrier(
        (student_hidden, teacher_hidden, first)
    )
    student_wide, teacher_wide = student_wide.astype(f32), teacher_wide.astype(f32)
    squares = jnp.stack(
        [jnp.sum(student_wide * student_wide, axis=1), jnp.sum(teacher_wide * teacher_wide, axis=1)]
    )
    squares = tok_sum(squares)
    widths = jnp.array([[student_width], [teacher_width]], f32)
    inverse = lax.rsqrt(squares / widths + epsilon)
    four = inverse.reshape(4, part_rows).T
    high = lax.reduce_precision(four, 8, 7)
    mid = lax.reduce_precision(four - high, 8, 7)
    pieces = jnp.concatenate([high, mid, four - high - mid], axis=1)
    pieces = jnp.pad(pieces, ((0, 0), (0, LANES - 12))).astype(jnp.bfloat16)
    student_b_own = jnp.concatenate([student_hidden[halves[1]], pieces], axis=1)
    targets = target_ids.reshape(blocks, own_rows)

    def mine(x):
        x = lax.dynamic_slice_in_dim(x, t * QUARTER, QUARTER)
        return jnp.concatenate([x, x]).reshape(1, LANES)

    def start(rows, gain, head, dep):
        keep_p, send_p, keep_q, send_q = partial_logits(t_arr, rows, gain, head, (0, 1), dep)
        gots = (lax.ppermute(send_p, "tok", TOK_X), lax.ppermute(send_q, "tok", TOK_Y))
        return gots, (keep_p, keep_q), keep_q

    def onward(gots, keeps, head, dep):
        next_p, own_p, next_q, own_q = relay(gots, keeps, logits_tile(head), dep)
        last_p = lax.ppermute(next_p, "tok", TOK_Y)
        last_q = lax.ppermute(next_q, "tok", TOK_X)
        return (own_p, own_q), (last_p, last_q), own_q

    def share(grad):
        gx = lax.ppermute(grad, "tok", TOK_X)
        gy = lax.ppermute(grad, "tok", TOK_Y)
        corner = (gx[:, :half], gy[:, half:])
        dp = lax.ppermute(corner[0], "tok", TOK_Y)
        dq = lax.ppermute(corner[1], "tok", TOK_X)
        return (grad, gx, gy, dp, dq), corner[0]

    row_targets = [mine(targets[:, rows].reshape(-1)) for rows in halves]

    student, teacher = (student_gain, student_head), (teacher_gain, teacher_head)
    gots_sa, keeps_sa, dep = start(student_a, *student, base)
    student_b = gather_rows(student_b_own, dep)
    gots_ta, keeps_ta, dep = start(teacher_a, *teacher, dep)
    own_sa, last_sa, dep = onward(gots_sa, keeps_sa, student_head, dep)
    teacher_b = gather_rows(teacher_hidden[halves[1]], dep)
    gots_sb, keeps_sb, dep = start(student_b, *student, dep)
    pieces = student_b[:, student_hidden.shape[1] :].astype(f32)
    pieces = (pieces[:, 0:4] + pieces[:, 4:8]) + pieces[:, 8:12]
    inv_s, inv_t = [mine(pieces[:, k]) for k in (0, 1)], [mine(pieces[:, k]) for k in (2, 3)]
    logits_sa, stats = finish(
        student_kernel, own_sa, last_sa, inv_s[0], (row_targets[0], base), dep
    )
    own_ta, last_ta, dep = onward(gots_ta, keeps_ta, teacher_head, stats)
    gots_tb, keeps_tb, dep = start(teacher_b, *teacher, dep)
    logits_ta, stats_a = finish(
        teacher_kernel, own_ta, last_ta, inv_t[0], (logits_sa, stats), dep
    )
    own_sb, last_sb, dep = onward(gots_sb, keeps_sb, student_head, stats_a)
    all_a = range_gather(stats_a, False)
    own_tb, last_tb, dep = onward(gots_tb, keeps_tb, teacher_head, dep)
    grad_a, loss_a = slope(base, logits_sa, logits_ta, all_a, row_targets[0], dep)
    grads_a, corner = share(grad_a)
    logits_sb, stats = finish(
        student_kernel, own_sb, last_sb, inv_s[1], (row_targets[1], base), grad_a
    )
    logits_tb, stats_b = finish(
        teacher_kernel, own_tb, last_tb, inv_t[1], (logits_sb, stats), stats
    )
    all_b = range_gather(stats_b, False)
    grad_b, loss_b = slope(base, logits_sb, logits_tb, all_b, row_targets[1], corner)
    grads_b, _ = share(grad_b)

    infos = range_gather(jnp.stack([loss_a, loss_b]), False)
    inner = tree_sum([infos[k, :, 1, :QUARTER] for k in range(blocks)])
    losses = loss_a[0, :QUARTER] + loss_b[0, :QUARTER]
    shared = jnp.concatenate([inner, losses[None]])
    sets = [shared] + [lax.ppermute(shared, "tok", way) for way in (TOK_X, TOK_Y, TOK_D)]
    loss = jnp.sum(((sets[0] + sets[1]) + (sets[2] + sets[3]))[2]) / all_rows
    me = lax.axis_index(("grp", "vocab"))
    holder = me * part_rows // QUARTER
    inner = lax.dynamic_index_in_dim(jnp.stack(sets), jnp.bitwise_xor(t, holder), 0, False)
    inner = lax.dynamic_slice_in_dim(inner[:2], me * part_rows % QUARTER, part_rows, 1)
    own_inv = inverse[0]
    scale = [own_inv[rows] ** 2 * inner[n] / student_width for n, rows in enumerate(halves)]

    flip = lax.axis_index("grp").astype(jnp.int32).reshape(1) * int(small_box())

    def result(grads, part, dep):
        rows = halves[part]
        hidden, inv = student_hidden[rows], own_inv[rows]
        mine, other = norm_gradient(t_arr, flip, *grads, student_head, dep)
        if small_box():
            other = lax.ppermute(other, "grp", SWAP)
            z = lax.axis_index("vocab").astype(jnp.int32).reshape(1)
            own, *sends = fold(z, mine, other)
            gots = [
                lax.ppermute(x, "vocab", [(i, i ^ k) for i in range(4)])
                for k, x in enumerate(sends, 1)
            ]
            return last(own, gots, hidden, student_gain, inv, scale[part]), own
        norm = jnp.concatenate([mine, other])
        norm = lax.psum_scatter(norm, ("grp", "vocab"), scatter_dimension=0, tiled=True)
        out = inv[:, None] * student_gain * norm - hidden.astype(f32) * scale[part][:, None]
        return out.astype(jnp.bfloat16), mine

    out_a, dep = result(grads_a, 0, grad_b)
    out_b, _ = result(grads_b, 1, dep)
    return (loss, jnp.concatenate([out_a, out_b]))


def solution(mesh):
    in_specs = (
        P(("grp", "vocab"), "tok"),
        P(("grp", "vocab"), "tok"),
        P("tok"),
        P("tok"),
        P(("grp", "vocab"), "tok"),
        P(("grp", "vocab"), "tok"),
        P(),
    )
    out_specs = (P(), P(("grp", "vocab"), "tok"))
    return jax.shard_map(
        on_device, mesh=mesh, in_specs=in_specs, out_specs=out_specs, check_vma=False
    )
```

```python
import functools
import jax
import jax.numpy as jnp
from jax import lax
from jax.experimental import pallas as pl
from jax.experimental.pallas import tpu as pltpu
from jax.sharding import PartitionSpec as P

heat = 2.0
blend = 0.5
grad_scale = 1024.0
epsilon = 1e-05

f32 = jnp.float32
VMEM_LIMIT = 56 * 1024 * 1024
LANES = 128
QUARTER = LANES // 2
PAD = 16
BLOCK_BYTES = 8 * 1024 * 1024

TOK_X = [(i, i ^ 1) for i in range(4)]
TOK_Y = [(i, i ^ 2) for i in range(4)]
TOK_D = [(i, i ^ 3) for i in range(4)]
SWAP = [(0, 1), (1, 0)]

VMEM = pl.BlockSpec(memory_space=pltpu.VMEM)
SMEM = pl.BlockSpec(memory_space=pltpu.SMEM)
ANY = pl.BlockSpec(memory_space=pl.ANY)
PARAMS = pltpu.CompilerParams(vmem_limit_bytes=VMEM_LIMIT)


LIGHT = pl.CostEstimate(flops=1024, bytes_accessed=1024, transcendentals=0)


def pow2(k):
    one = jnp.ones_like(k)
    a = jnp.left_shift(one, jnp.clip(k + 60, 0, 30)).astype(f32)
    b = jnp.left_shift(one, jnp.clip(k + 30, 0, 30)).astype(f32)
    c = jnp.left_shift(one, jnp.clip(k, 0, 30)).astype(f32)
    d = jnp.left_shift(one, jnp.clip(k - 30, 0, 30)).astype(f32)
    return (a * (2.0**-60)) * b * c * d


def encode(x):
    top = jnp.max(jnp.abs(x), axis=0, keepdims=True)
    e = jnp.ceil(jnp.log2(jnp.maximum(top, 2.0**-44))).astype(jnp.int32)
    e = jnp.clip(e, -44, 31)
    q = jnp.clip(jnp.round(x * pow2(15 - e)), -32767.0, 32767.0)
    return q.astype(jnp.int32).astype(jnp.int16), e


def decode(q, e):
    return q.astype(jnp.int32).astype(f32) * pow2(e - 15)


def low_lanes(shape):
    return lax.broadcasted_iota(jnp.int32, shape, 1) < QUARTER


def swap_lanes(x):
    return pltpu.roll(x, QUARTER, 1)


def row_is(shape, j):
    return lax.broadcasted_iota(jnp.int32, shape, 0) == j


ORDER = ((0, 2, 1, 3), (0, 1, 2, 3))


def logits_kernel(parts, tiles, tile, t_ref, rows_ref, gain_ref, h_ref, dep_ref, *refs):
    outs, (a_ref, exps) = refs[: 2 * len(parts)], refs[2 * len(parts) :]
    j = pl.program_id(0)

    @pl.when(j == 0)
    def _():
        t = t_ref[0]
        for k in range(4):
            place = pl.multiple_of(jnp.bitwise_xor(t, k) * QUARTER, QUARTER)
            w = rows_ref[pl.ds(place, QUARTER), :].astype(f32) * gain_ref[...]
            w = w.astype(jnp.bfloat16)
            for n, part in enumerate(parts):
                at = ORDER[part].index(k) * QUARTER
                a_ref[n, at : at + QUARTER, :] = w

    for n in range(len(parts)):
        keep_ref, send_ref = outs[2 * n], outs[2 * n + 1]
        half = send_ref.shape[0] - PAD

        @pl.when((j >= n * tiles) & (j < (n + 1) * tiles))
        def _():
            r = lax.dot_general(
                h_ref[...], a_ref[n], (((1,), (1,)), ((), ())), preferred_element_type=f32
            )
            keep_ref[...] = r[:, :LANES]
            q, e = encode(r[:, LANES:])
            at = j - n * tiles
            send_ref[pl.ds(pl.multiple_of(at * tile, tile), tile), :] = q
            before = jnp.where(at == 0, 0, exps[...])
            exps[...] = jnp.where(row_is((PAD, LANES), at), e, before)

            @pl.when(at == tiles - 1)
            def _():
                send_ref[half:, :] = exps[...].astype(jnp.int16)


def logits_tile(head):
    return min(BLOCK_BYTES // (2 * head.shape[1]), head.shape[0] // 2)


def partial_logits(t, rows, gain, head, parts, dep):
    count, width = rows.shape[0], head.shape[1]
    half = head.shape[0] // 2
    tile = logits_tile(head)
    tiles = half // tile
    first = parts[0] * tiles
    out_specs, out_shape = [], []
    for n in range(len(parts)):
        out_specs += [
            pl.BlockSpec(
                (tile, LANES), lambda j, n=n: (jnp.clip(j - n * tiles, 0, tiles - 1), 0)
            ),
            pl.BlockSpec((half + PAD, LANES), lambda j: (0, 0)),
        ]
        out_shape += [
            jax.ShapeDtypeStruct((half, LANES), f32),
            jax.ShapeDtypeStruct((half + PAD, LANES), jnp.int16),
        ]
    return pl.pallas_call(
        functools.partial(logits_kernel, parts, tiles, tile),
        grid=(len(parts) * tiles,),
        in_specs=[
            SMEM,
            pl.BlockSpec((count, width), lambda j: (0, 0)),
            pl.BlockSpec((1, width), lambda j: (0, 0)),
            pl.BlockSpec((tile, width), lambda j: (first + j, 0)),
            ANY,
        ],
        out_specs=out_specs,
        out_shape=out_shape,
        scratch_shapes=[
            pltpu.VMEM((len(parts), count, width), jnp.bfloat16),
            pltpu.VMEM((PAD, LANES), jnp.int32),
        ],
        compiler_params=PARAMS,
        cost_estimate=LIGHT,
        name="logits",
    )(t, rows, gain.reshape(1, width), head, dep)


def relay_kernel(step, tile, *refs):
    ins, outs, news = refs[:11], refs[11:15], refs[15:]
    n, steps = pl.program_id(0), pl.num_programs(0)
    for p in range(2):
        got_top, got_low, exps_ref, keep_top, keep_low = ins[5 * p : 5 * p + 5]
        next_ref, own_ref, new = outs[2 * p], outs[2 * p + 1], news[p]
        exps = exps_ref[...].astype(jnp.int32)

        def exponent(at):
            here = row_is(exps.shape, at // tile)
            return jnp.sum(jnp.where(here, exps, 0), axis=0, keepdims=True)

        top = keep_top[...] + decode(got_top[...], exponent(n * step))
        low = keep_low[...] + decode(got_low[...], exponent((steps + n) * step))
        mask = low_lanes(top.shape)
        own_ref[...] = jnp.where(mask, top, swap_lanes(low))
        q, e = encode(jnp.where(mask, swap_lanes(top), low))
        next_ref[pl.ds(pl.multiple_of(n * step, step), step), :] = q
        before = jnp.where(n == 0, 0, new[...])
        new[...] = jnp.where(row_is(new.shape, n), e, before)

        @pl.when(n == steps - 1)
        def _():
            next_ref[steps * step :, :] = new[...].astype(jnp.int16)


def relay(gots, keeps, tile, dep):
    half = keeps[0].shape[0]
    step = min(512, half // 2)
    steps = half // 2 // step
    top = pl.BlockSpec((step, LANES), lambda n: (n, 0))
    low = pl.BlockSpec((step, LANES), lambda n: (steps + n, 0))
    exps = pl.BlockSpec((PAD, LANES), lambda n: (half // PAD, 0))
    shapes = [
        jax.ShapeDtypeStruct((half // 2 + PAD, LANES), jnp.int16),
        jax.ShapeDtypeStruct((half // 2, LANES), f32),
    ]
    operands = []
    for got, keep in zip(gots, keeps):
        operands += [got, got, got, keep, keep]
    return pl.pallas_call(
        functools.partial(relay_kernel, step, tile),
        grid=(steps,),
        in_specs=[top, low, exps, top, low] * 2 + [ANY],
        out_specs=[pl.BlockSpec((half // 2 + PAD, LANES), lambda n: (0, 0)), top] * 2,
        out_shape=shapes * 2,
        scratch_shapes=[pltpu.VMEM((PAD, LANES), jnp.int32)] * 2,
        compiler_params=PARAMS,
        cost_estimate=LIGHT,
        name="relay",
    )(*operands, dep)


def inverse_norms(pieces_ref, k):
    x = pieces_ref[...].astype(f32)
    x = jnp.transpose(jnp.concatenate([x, x], axis=0))
    return (x[k : k + 1] + x[k + 4 : k + 5]) + x[k + 8 : k + 9]


def merged(op, x):
    return op(x, swap_lanes(x))


def summed(owns, lasts, inv, out_ref):
    top = None
    for p in range(2):
        packed = owns[p].shape[0]
        step = min(512, packed)
        exps = lasts[p][packed : packed + PAD, :].astype(jnp.int32)
        for n in range(packed // step):
            rows = slice(n * step, (n + 1) * step)
            x = owns[p][rows, :] + decode(lasts[p][rows, :], exps[n : n + 1, :])
            x = x * inv
            out_ref[p * packed + n * step : p * packed + (n + 1) * step, :] = x
            high = jnp.max(x, axis=0, keepdims=True)
            top = high if top is None else jnp.maximum(top, high)
    return merged(jnp.maximum, top)


def places(shape, at, packed):
    part, start = at // packed, at % packed
    row = lax.broadcasted_iota(jnp.int32, shape, 0) + (2 * part * packed + start)
    return jnp.where(low_lanes(shape), row, row + packed)


def student_kernel(k, op, oq, lp, lq, inv_ref, target_ref, base_ref, dep, out_ref, stats_ref):
    packed = op.shape[0]
    step = min(512, packed)
    top = summed((op, oq), (lp, lq), inverse_norms(inv_ref, k), out_ref)
    soft = jnp.zeros((1, LANES), f32)
    plain = jnp.zeros((1, LANES), f32)
    hit = jnp.zeros((1, LANES), f32)
    target = target_ref[...] - base_ref[0]
    for n in range(2 * packed // step):
        x = out_ref[n * step : (n + 1) * step, :]
        warm = jnp.exp((x - top) * (1.0 / heat))
        soft = soft + jnp.sum(warm, axis=0, keepdims=True)
        plain = plain + jnp.sum(warm * warm, axis=0, keepdims=True)
        here = places(x.shape, n * step, packed) == target
        hit = hit + jnp.sum(jnp.where(here, x, 0.0), axis=0, keepdims=True)
    stats = jnp.zeros((8, LANES), f32)
    sums = [merged(jnp.add, v) for v in (soft, plain, hit)]
    for n, value in enumerate([top] + sums):
        stats = jnp.where(row_is(stats.shape, n), value, stats)
    stats_ref[...] = stats


def teacher_kernel(k, op, oq, lp, lq, inv_ref, student_ref, before_ref, dep, out_ref, stats_ref):
    packed = op.shape[0]
    step = min(512, packed)
    top = summed((op, oq), (lp, lq), inverse_norms(inv_ref, k), out_ref)
    top = top * (1.0 / heat)
    total = jnp.zeros((1, LANES), f32)
    cross = jnp.zeros((1, LANES), f32)
    for n in range(2 * packed // step):
        rows = slice(n * step, (n + 1) * step)
        x = out_ref[rows, :]
        power = jnp.exp(x * (1.0 / heat) - top)
        total = total + jnp.sum(power, axis=0, keepdims=True)
        gap = (x - student_ref[rows, :]) * (1.0 / heat)
        cross = cross + jnp.sum(power * gap, axis=0, keepdims=True)
    stats = before_ref[...]
    sums = [merged(jnp.add, v) for v in (total, cross)]
    for n, value in enumerate([top] + sums):
        stats = jnp.where(row_is(stats.shape, 4 + n), value, stats)
    stats_ref[...] = stats


def finish(body, k, owns, lasts, inv, extra, dep):
    packed = owns[0].shape[0]
    last_spec = SMEM if body is student_kernel else VMEM
    return pl.pallas_call(
        functools.partial(body, k),
        in_specs=[VMEM] * 6 + [last_spec, ANY],
        out_specs=[VMEM] * 2,
        out_shape=[
            jax.ShapeDtypeStruct((2 * packed, LANES), f32),
            jax.ShapeDtypeStruct((8, LANES), f32),
        ],
        compiler_params=PARAMS,
        cost_estimate=LIGHT,
        name="finish",
    )(*owns, *lasts, inv, *extra, dep)


def tree_sum(parts):
    while len(parts) > 1:
        parts = [a + b for a, b in zip(parts[::2], parts[1::2])]
    return parts[0]


def thirds(x):
    high = x.astype(jnp.bfloat16).astype(f32)
    mid = (x - high).astype(jnp.bfloat16).astype(f32)
    return [high, mid, x - high - mid]


def slope_kernel(
    student_ref, teacher_ref, stats_ref, target_ref, base_ref, dep, grad_ref
):
    packed = student_ref.shape[0] // 2
    step = min(512, packed)
    sets = [stats_ref[k] for k in range(stats_ref.shape[0])]
    top = functools.reduce(jnp.maximum, sets)

    def scaled(row, top_row, rate):
        high = top[top_row : top_row + 1]
        return tree_sum(
            [s[row : row + 1] * jnp.exp((s[top_row : top_row + 1] - high) * rate) for s in sets]
        )

    student_top, teacher_top = top[0:1], top[4:5]
    soft_total = scaled(1, 0, 1.0 / heat)
    plain_total = scaled(2, 0, 1.0)
    teacher_total = scaled(5, 4, 1.0)
    cross_total = scaled(6, 4, 1.0)
    label = tree_sum([s[3:4] for s in sets])
    row_loss = blend * heat**2 * (
        cross_total / teacher_total
        - teacher_top
        - jnp.log(teacher_total)
        + student_top / heat
        + jnp.log(soft_total)
    ) + (1.0 - blend) * (student_top + jnp.log(plain_total) - label)
    soft_rate = grad_scale * blend * heat / soft_total
    teacher_rate = grad_scale * blend * heat / teacher_total
    plain_rate = grad_scale * (1.0 - blend) / plain_total
    inner = jnp.zeros((1, LANES), f32)
    target = target_ref[...] - base_ref[0]
    for n in range(2 * packed // step):
        rows = slice(n * step, (n + 1) * step)
        logits = student_ref[rows, :]
        warm = jnp.exp((logits - student_top) * (1.0 / heat))
        power = jnp.exp(teacher_ref[rows, :] * (1.0 / heat) - teacher_top)
        g = warm * (soft_rate + plain_rate * warm) - power * teacher_rate
        here = places(g.shape, n * step, packed) == target
        g = jnp.where(here, g - grad_scale * (1.0 - blend), g)
        g = g.astype(jnp.bfloat16).astype(f32)
        inner = inner + jnp.sum(g * logits, axis=0, keepdims=True)
        g = jnp.transpose(g).astype(jnp.bfloat16)
        at = 2 * (n * step // packed) * packed + (n * step) % packed
        grad_ref[:, at : at + step] = g[:QUARTER]
        grad_ref[:, at + packed : at + packed + step] = g[QUARTER:]
    extra = jnp.zeros((LANES, LANES), f32)
    for n, value in enumerate(thirds(merged(jnp.add, inner)) + thirds(row_loss)):
        extra = jnp.where(row_is(extra.shape, n), value, extra)
    extra = jnp.transpose(extra).astype(jnp.bfloat16)
    grad_ref[:, 2 * 2 * packed :] = extra[:QUARTER]


def slope(base, student, teacher, stats, targets, dep):
    return pl.pallas_call(
        slope_kernel,
        in_specs=[VMEM] * 4 + [SMEM, ANY],
        out_specs=VMEM,
        out_shape=jax.ShapeDtypeStruct((QUARTER, 2 * student.shape[0] + LANES), jnp.bfloat16),
        compiler_params=PARAMS,
        cost_estimate=LIGHT,
        name="slope",
    )(student, teacher, stats, targets, base, dep)


def norm_grad_kernel(t_ref, flip_ref, own, gx, gy, dp, dq, h_ref, dep, keep, send, loss, lhs):
    vocab, tile = h_ref.shape
    half = dp.shape[1]
    j = pl.program_id(0)
    t = jnp.bitwise_xor(t_ref[0], 2 * flip_ref[0])

    def place(n, columns, value):
        quarter = jnp.bitwise_xor(t, n)
        at = pl.ds(pl.multiple_of(lax.rem(quarter, 2) * QUARTER, QUARTER), QUARTER)

        @pl.when(quarter < 2)
        def _():
            keep[at, columns] = value

        @pl.when(quarter >= 2)
        def _():
            send[at, columns] = value

    @pl.when(j == 0)
    def _():
        for n, ref in enumerate((own, gx, gy)):
            lhs[n * QUARTER : (n + 1) * QUARTER, :] = ref[:, :vocab]
        lhs[3 * QUARTER :, :half] = dp[...]
        lhs[3 * QUARTER :, half:] = dq[:, : vocab - half]
        losses = []
        for n, ref in enumerate((own, gx, gy, dq)):
            x = ref[:, ref.shape[1] - LANES :].astype(f32)
            lane = lax.broadcasted_iota(jnp.int32, x.shape, 1)
            inner = jnp.sum(jnp.where(lane < 3, x, 0.0), axis=1, keepdims=True)
            place(n, slice(keep.shape[1] - LANES, keep.shape[1]), jnp.broadcast_to(inner, x.shape))
            x = jnp.where((lane >= 3) & (lane < 6), x, 0.0)
            losses.append(jnp.sum(jnp.sum(x, axis=1, keepdims=True), axis=0, keepdims=True))
        loss[...] = jnp.broadcast_to(tree_sum(losses), loss.shape)

    r = jnp.dot(lhs[...], h_ref[...], preferred_element_type=f32)
    columns = pl.ds(pl.multiple_of(j * tile, tile), tile)
    for n in range(4):
        place(n, columns, r[n * QUARTER : (n + 1) * QUARTER])


def norm_gradient(t, flip, own, gx, gy, dp, dq, head, dep):
    vocab, width = head.shape
    tile = min(512, width)
    parts = (own, gx, gy, dp, dq)
    rows = jax.ShapeDtypeStruct((2 * QUARTER, width + LANES), f32)
    return pl.pallas_call(
        norm_grad_kernel,
        grid=(width // tile,),
        in_specs=[SMEM, SMEM]
        + [pl.BlockSpec(x.shape, lambda j: (0, 0)) for x in parts]
        + [pl.BlockSpec((vocab, tile), lambda j: (0, j)), ANY],
        out_specs=[pl.BlockSpec(rows.shape, lambda j: (0, 0))] * 2
        + [pl.BlockSpec((8, LANES), lambda j: (0, 0))],
        out_shape=[rows, rows, jax.ShapeDtypeStruct((8, LANES), f32)],
        scratch_shapes=[pltpu.VMEM((4 * QUARTER, vocab), jnp.bfloat16)],
        compiler_params=PARAMS,
        cost_estimate=LIGHT,
        name="norm_grad",
    )(t, flip, *parts, head, dep)


def exponent(top):
    e = jnp.ceil(jnp.log2(jnp.maximum(top, 2.0**-44))).astype(jnp.int32)
    return jnp.clip(e, -44, 44)


def fold_kernel(z_ref, mine_ref, other_ref, dep_p, dep_q, own_ref, *sends):
    rows, width = own_ref.shape[0], own_ref.shape[1] - LANES
    for k in range(4):
        at = pl.ds(pl.multiple_of(jnp.bitwise_xor(z_ref[0], k) * rows, rows), rows)
        x = mine_ref[at, :] + other_ref[at, :]
        if k == 0:
            own_ref[...] = x
            continue
        norm, inner = x[:, :width], x[:, width:]
        e = exponent(jnp.max(jnp.abs(norm), axis=1, keepdims=True))
        q = jnp.clip(jnp.round(norm * pow2(15 - e)), -32767.0, 32767.0)
        sends[k - 1][:, :width] = q.astype(jnp.int32).astype(jnp.int16)
        e_inner = exponent(jnp.abs(inner))
        inner = jnp.clip(inner * pow2(15 - e_inner), -32767.0, 32767.0)
        high = jnp.round(inner)
        low = jnp.round((inner - high) * 32768.0)
        lane = lax.broadcasted_iota(jnp.int32, inner.shape, 1)
        tail = jnp.where(lane == 0, jnp.broadcast_to(e, inner.shape), e_inner)
        tail = jnp.where(lane == 2, high.astype(jnp.int32), tail)
        tail = jnp.where(lane == 3, low.astype(jnp.int32), tail)
        sends[k - 1][:, width:] = tail.astype(jnp.int16)


def fold(z, mine, other, deps):
    rows, width = other.shape
    return pl.pallas_call(
        fold_kernel,
        in_specs=[SMEM, VMEM, VMEM, ANY, ANY],
        out_specs=[VMEM] * 4,
        out_shape=[jax.ShapeDtypeStruct((rows // 4, width), f32)]
        + [jax.ShapeDtypeStruct((rows // 4, width), jnp.int16)] * 3,
        compiler_params=PARAMS,
        cost_estimate=LIGHT,
        name="fold",
    )(z, mine, other, *deps)


def last_kernel(features, own_ref, p1, p2, p3, hidden_ref, gain_ref, inv_ref, before, out_ref):
    width = hidden_ref.shape[1]
    norm, inner = own_ref[:, :width], own_ref[:, width : width + 1]
    for p in (p1, p2, p3):
        tail = p[:, width:].astype(jnp.int32)
        norm = norm + p[:, :width].astype(jnp.int32).astype(f32) * pow2(tail[:, 0:1] - 15)
        value = tail[:, 2:3].astype(f32) + tail[:, 3:4].astype(f32) * (1.0 / 32768.0)
        inner = inner + value * pow2(tail[:, 1:2] - 15)
    inv = inv_ref[:, :1]
    scale = inv * inv * inner * (1.0 / features)
    out = inv * gain_ref[...] * norm - hidden_ref[...].astype(f32) * scale
    out_ref[...] = out.astype(jnp.bfloat16)


def last(features, own, gots, hidden, gain, inv, part, before):
    count, width = own.shape[0], hidden.shape[1]
    block = pl.BlockSpec((count, width), lambda j: (part, 0))
    given = before is not None
    return pl.pallas_call(
        functools.partial(last_kernel, features),
        grid=(1,),
        in_specs=[VMEM] * 4
        + [block, VMEM, pl.BlockSpec((count, LANES), lambda j: (part, 0)), ANY],
        out_specs=block,
        out_shape=jax.ShapeDtypeStruct(hidden.shape, jnp.bfloat16),
        input_output_aliases={7: 0} if given else {},
        compiler_params=PARAMS,
        cost_estimate=LIGHT,
        name="hidden_grad",
    )(own, *gots, hidden, gain.reshape(1, -1), inv, before if given else inv)


def tie(x, *others):
    return lax.optimization_barrier((x, *others))[0]


def tok_sum(x):
    a = lax.ppermute(x, "tok", TOK_X)
    b = lax.ppermute(x, "tok", TOK_Y)
    c = lax.ppermute(x, "tok", TOK_D)
    return (x + a) + (b + c)


def small_box():
    return lax.axis_size("grp") == 2 and lax.axis_size("vocab") == 4


def along_z(x):
    return [x] + [lax.ppermute(x, "vocab", [(i, i ^ k) for i in range(4)]) for k in range(1, 4)]


def range_gather(x, ordered):
    if not small_box():
        return lax.all_gather(x, ("grp", "vocab"), axis=0)
    own = jnp.stack(along_z(x))
    sets = jnp.concatenate([own, lax.ppermute(own, "grp", SWAP)])
    if ordered:
        sets = sets[jnp.bitwise_xor(lax.axis_index(("grp", "vocab")), jnp.arange(8))]
    return sets


def on_device(
    teacher_hidden,
    student_hidden,
    teacher_gain,
    student_gain,
    teacher_head,
    student_head,
    target_ids,
):
    blocks = lax.axis_size("grp") * lax.axis_size("vocab")
    own_rows = teacher_hidden.shape[0]
    all_rows = blocks * own_rows
    part_rows = own_rows // 2
    vocab_local = teacher_head.shape[0]
    half = vocab_local // 2
    teacher_width = teacher_hidden.shape[1] * lax.axis_size("tok")
    student_width = student_hidden.shape[1] * lax.axis_size("tok")
    t = lax.axis_index("tok")
    t_arr = t.astype(jnp.int32).reshape(1)
    base = (lax.axis_index(("grp", "vocab")) * vocab_local).astype(jnp.int32).reshape(1)

    halves = [slice(0, part_rows), slice(part_rows, own_rows)]

    def gather_rows(x, after=None):
        if after is not None:
            x, _ = lax.optimization_barrier((x, after))
        return lax.all_gather(x, ("grp", "vocab"), axis=0, tiled=True)

    if small_box():
        near = along_z(student_hidden[halves[0]])
        sets = jnp.stack(near)
        sets = jnp.concatenate([sets, lax.ppermute(sets, "grp", SWAP)])
        place = jnp.bitwise_xor(lax.axis_index(("grp", "vocab")), jnp.arange(blocks))
        student_a = sets[place].reshape(blocks * part_rows, -1)
        first = near[1]
    else:
        student_a = gather_rows(student_hidden[halves[0]])
        first = student_a
    teacher_a = gather_rows(teacher_hidden[halves[0]], first)

    student_wide, teacher_wide, _ = lax.optimization_barrier(
        (student_hidden, teacher_hidden, first)
    )
    student_wide, teacher_wide = student_wide.astype(f32), teacher_wide.astype(f32)
    squares = jnp.stack(
        [jnp.sum(student_wide * student_wide, axis=1), jnp.sum(teacher_wide * teacher_wide, axis=1)]
    )
    squares = tok_sum(squares)
    widths = jnp.array([[student_width], [teacher_width]], f32)
    inverse = lax.rsqrt(squares / widths + epsilon)
    four = inverse.reshape(4, part_rows).T
    high = lax.reduce_precision(four, 8, 7)
    mid = lax.reduce_precision(four - high, 8, 7)
    pieces = jnp.concatenate([high, mid, four - high - mid], axis=1)
    pieces = jnp.pad(pieces, ((0, 0), (0, LANES - 12))).astype(jnp.bfloat16)
    student_b_own = jnp.concatenate([student_hidden[halves[1]], pieces], axis=1)
    targets = target_ids.reshape(blocks, own_rows)

    def mine(x):
        x = lax.dynamic_slice_in_dim(x, t * QUARTER, QUARTER)
        return jnp.concatenate([x, x]).reshape(1, LANES)

    def start(rows, gain, head, dep):
        keep_p, send_p, keep_q, send_q = partial_logits(t_arr, rows, gain, head, (0, 1), dep)
        gots = (lax.ppermute(send_p, "tok", TOK_X), lax.ppermute(send_q, "tok", TOK_Y))
        return gots, (keep_p, keep_q), keep_q

    def onward(gots, keeps, head, dep):
        next_p, own_p, next_q, own_q = relay(gots, keeps, logits_tile(head), dep)
        last_p = lax.ppermute(next_p, "tok", TOK_Y)
        last_q = lax.ppermute(next_q, "tok", TOK_X)
        return (own_p, own_q), (last_p, last_q), own_q

    def share(grad):
        gx = lax.ppermute(grad, "tok", TOK_X)
        gy = lax.ppermute(grad, "tok", TOK_Y)
        corner = (gx[:, :half], gy[:, half:])
        dp = lax.ppermute(corner[0], "tok", TOK_Y)
        dq = lax.ppermute(corner[1], "tok", TOK_X)
        return (grad, gx, gy, dp, dq), corner

    row_targets = [mine(targets[:, rows].reshape(-1)) for rows in halves]

    student, teacher = (student_gain, student_head), (teacher_gain, teacher_head)
    gots_sa, keeps_sa, dep = start(student_a, *student, tie(base, *row_targets))
    student_b = gather_rows(student_b_own, dep)
    gots_ta, keeps_ta, dep = start(teacher_a, *teacher, dep)
    own_sa, last_sa, dep = onward(gots_sa, keeps_sa, student_head, dep)
    teacher_b = gather_rows(teacher_hidden[halves[1]], dep)
    gots_sb, keeps_sb, dep = start(student_b, *student, dep)
    pieces = student_b[:, student_hidden.shape[1] :]
    pieces = lax.dynamic_slice_in_dim(pieces, t * QUARTER, QUARTER)
    own_ta, last_ta, dep = onward(gots_ta, keeps_ta, teacher_head, tie(dep, pieces))
    gots_tb, keeps_tb, dep = start(teacher_b, *teacher, dep)
    logits_sa, stats = finish(
        student_kernel, 0, own_sa, last_sa, pieces, (row_targets[0], base), dep
    )
    own_sb, last_sb, dep = onward(gots_sb, keeps_sb, student_head, stats)
    logits_ta, stats_a = finish(
        teacher_kernel, 2, own_ta, last_ta, pieces, (logits_sa, stats), dep
    )
    all_a = range_gather(stats_a, False)
    own_tb, last_tb, dep = onward(gots_tb, keeps_tb, teacher_head, stats_a)
    grad_a = slope(base, logits_sa, logits_ta, all_a, row_targets[0], dep)
    grads_a, corner = share(grad_a)
    logits_sb, stats = finish(
        student_kernel, 1, own_sb, last_sb, pieces, (row_targets[1], base), grad_a
    )
    logits_tb, stats_b = finish(
        teacher_kernel, 3, own_tb, last_tb, pieces, (logits_sb, stats), stats
    )
    all_b = range_gather(stats_b, False)
    dep = tie(stats_b, *corner)
    grad_b = slope(base, logits_sb, logits_tb, all_b, row_targets[1], dep)
    grads_b, corner = share(grad_b)

    own_inv = jnp.broadcast_to(inverse[0][:, None], (own_rows, LANES))
    flip = lax.axis_index("grp").astype(jnp.int32).reshape(1) * int(small_box())

    def result(grads, part, dep, fold_deps, before):
        mine, other, loss = norm_gradient(t_arr, flip, *grads, student_head, dep)
        if small_box():
            other = lax.ppermute(other, "grp", SWAP)
            z = lax.axis_index("vocab").astype(jnp.int32).reshape(1)
            own, *sends = fold(z, mine, other, fold_deps)
            gots = [
                lax.ppermute(x, "vocab", [(i, i ^ k) for i in range(4)])
                for k, x in enumerate(sends, 1)
            ]
            out = last(
                student_width, own, gots, student_hidden, student_gain, own_inv, part, before
            )
            return out, loss, out
        norm = jnp.concatenate([mine, other])
        norm = lax.psum_scatter(norm, ("grp", "vocab"), scatter_dimension=0, tiled=True)
        at, width = halves[part], student_hidden.shape[1]
        inv, inner = own_inv[at, :1], norm[:, width : width + 1]
        out = inv * student_gain * norm[:, :width]
        out = out - student_hidden[at].astype(f32) * (inv * inv * inner / student_width)
        return out.astype(jnp.bfloat16), loss, mine

    dep = tie(grad_b, own_inv)
    out, loss_a, dep = result(grads_a, 0, dep, corner, None)
    second, loss_b, _ = result(grads_b, 1, dep, (t_arr, t_arr), out)
    loss = (loss_a[0, 0] + loss_b[0, 0]) / all_rows
    return (loss, second if small_box() else jnp.concatenate([out, second]))


def solution(mesh):
    in_specs = (
        P(("grp", "vocab"), "tok"),
        P(("grp", "vocab"), "tok"),
        P("tok"),
        P("tok"),
        P(("grp", "vocab"), "tok"),
        P(("grp", "vocab"), "tok"),
        P(),
    )
    out_specs = (P(), P(("grp", "vocab"), "tok"))
    return jax.shard_map(
        on_device, mesh=mesh, in_specs=in_specs, out_specs=out_specs, check_vma=False
    )
```

```python
import functools
import jax
import jax.numpy as jnp
from jax import lax
from jax.experimental import pallas as pl
from jax.experimental.pallas import tpu as pltpu
from jax.sharding import PartitionSpec as P

heat = 2.0
blend = 0.5
grad_scale = 1024.0
epsilon = 1e-05

f32 = jnp.float32
VMEM_LIMIT = 56 * 1024 * 1024
LANES = 128
QUARTER = LANES // 2
PAD = 16
BLOCK_ROWS = 1024

TOK_X = [(i, i ^ 1) for i in range(4)]
TOK_Y = [(i, i ^ 2) for i in range(4)]
TOK_D = [(i, i ^ 3) for i in range(4)]
SWAP = [(0, 1), (1, 0)]

VMEM = pl.BlockSpec(memory_space=pltpu.VMEM)
SMEM = pl.BlockSpec(memory_space=pltpu.SMEM)
ANY = pl.BlockSpec(memory_space=pl.ANY)
PARAMS = pltpu.CompilerParams(vmem_limit_bytes=VMEM_LIMIT)


LIGHT = pl.CostEstimate(flops=1024, bytes_accessed=1024, transcendentals=0)


def pow2(k):
    one = jnp.ones_like(k)
    a = jnp.left_shift(one, jnp.clip(k + 60, 0, 30)).astype(f32)
    b = jnp.left_shift(one, jnp.clip(k + 30, 0, 30)).astype(f32)
    c = jnp.left_shift(one, jnp.clip(k, 0, 30)).astype(f32)
    d = jnp.left_shift(one, jnp.clip(k - 30, 0, 30)).astype(f32)
    return (a * (2.0**-60)) * b * c * d


def encode(x):
    top = jnp.max(jnp.abs(x), axis=0, keepdims=True)
    e = jnp.ceil(jnp.log2(jnp.maximum(top, 2.0**-44))).astype(jnp.int32)
    e = jnp.clip(e, -44, 31)
    q = jnp.clip(jnp.round(x * pow2(15 - e)), -32767.0, 32767.0)
    return q.astype(jnp.int32).astype(jnp.int16), e


def decode(q, e):
    return q.astype(jnp.int32).astype(f32) * pow2(e - 15)


def low_lanes(shape):
    return lax.broadcasted_iota(jnp.int32, shape, 1) < QUARTER


def swap_lanes(x):
    return pltpu.roll(x, QUARTER, 1)


def row_is(shape, j):
    return lax.broadcasted_iota(jnp.int32, shape, 0) == j


ORDER = ((0, 2, 1, 3), (0, 1, 2, 3))


def logits_kernel(tiles, tile, relay_tile, t_ref, rows_ref, gain_ref, h_ref, dep_ref, *refs):
    passed = relay_tile is not None
    ins, refs = (refs[:10], refs[10:]) if passed else ((), refs)
    outs, refs = refs[:4], refs[4:]
    onward, refs = (refs[:4], refs[4:]) if passed else ((), refs)
    a_ref, exps, *news = refs
    j = pl.program_id(0)

    @pl.when(j == 0)
    def _():
        t = t_ref[0]
        for k in range(4):
            place = pl.multiple_of(jnp.bitwise_xor(t, k) * QUARTER, QUARTER)
            w = rows_ref[pl.ds(place, QUARTER), :].astype(f32) * gain_ref[...]
            w = w.astype(jnp.bfloat16)
            for part in range(2):
                at = ORDER[part].index(k) * QUARTER
                a_ref[part, at : at + QUARTER, :] = w

    for part in range(2):
        keep_ref, send_ref = outs[2 * part], outs[2 * part + 1]
        half = send_ref.shape[0] - PAD
        at = j - part * tiles

        @pl.when((at >= 0) & (at < tiles))
        def _():
            r = lax.dot_general(
                h_ref[...], a_ref[part], (((1,), (1,)), ((), ())), preferred_element_type=f32
            )
            if passed:
                relay_step(
                    at,
                    tiles,
                    relay_tile,
                    ins[5 * part : 5 * part + 5],
                    *onward[2 * part : 2 * part + 2],
                    news[part],
                )
            keep_ref[...] = r[:, :LANES]
            q, e = encode(r[:, LANES:])
            send_ref[pl.ds(pl.multiple_of(at * tile, tile), tile), :] = q
            before = jnp.where(at == 0, 0, exps[...])
            exps[...] = jnp.where(row_is((PAD, LANES), at), e, before)

            @pl.when(at == tiles - 1)
            def _():
                send_ref[half:, :] = exps[...].astype(jnp.int16)


def logits_tile(head):
    return min(BLOCK_ROWS, head.shape[0] // 2)


def partial_logits(t, rows, gain, head, dep, pending=None):
    count, width = rows.shape[0], head.shape[1]
    half = head.shape[0] // 2
    tile = logits_tile(head)
    tiles = half // tile
    in_specs = [
        SMEM,
        pl.BlockSpec((count, width), lambda j: (0, 0)),
        pl.BlockSpec((1, width), lambda j: (0, 0)),
        pl.BlockSpec((tile, width), lambda j: (j, 0)),
        ANY,
    ]
    out_specs, out_shape, operands, extra = [], [], [], []
    ats = [lambda j, part=part: jnp.clip(j - part * tiles, 0, tiles - 1) for part in range(2)]
    for at in ats:
        out_specs += [
            pl.BlockSpec((tile, LANES), lambda j, at=at: (at(j), 0)),
            pl.BlockSpec((half + PAD, LANES), lambda j: (0, 0)),
        ]
        out_shape += [
            jax.ShapeDtypeStruct((half, LANES), f32),
            jax.ShapeDtypeStruct((half + PAD, LANES), jnp.int16),
        ]
    if pending is not None:
        operands = relay_operands(*pending)
        extra = [pltpu.VMEM((PAD, LANES), jnp.int32)] * 2
        for at in ats:
            ins, outs, shapes = relay_specs(half, tiles, at)
            in_specs += ins
            out_specs += outs
            out_shape += shapes
    return pl.pallas_call(
        functools.partial(logits_kernel, tiles, tile, None if pending is None else tile),
        grid=(2 * tiles,),
        in_specs=in_specs,
        out_specs=out_specs,
        out_shape=out_shape,
        scratch_shapes=[
            pltpu.VMEM((2, count, width), jnp.bfloat16),
            pltpu.VMEM((PAD, LANES), jnp.int32),
            *extra,
        ],
        compiler_params=PARAMS,
        cost_estimate=LIGHT,
        name="logits",
    )(t, rows, gain.reshape(1, width), head, dep, *operands)


def relay_step(n, steps, tile, ins, next_ref, own_ref, new):
    got_top, got_low, exps_ref, keep_top, keep_low = ins
    step = own_ref.shape[0]
    exps = exps_ref[...].astype(jnp.int32)

    def exponent_at(at):
        here = row_is(exps.shape, at // tile)
        return jnp.sum(jnp.where(here, exps, 0), axis=0, keepdims=True)

    top = keep_top[...] + decode(got_top[...], exponent_at(n * step))
    low = keep_low[...] + decode(got_low[...], exponent_at((steps + n) * step))
    mask = low_lanes(top.shape)
    own_ref[...] = jnp.where(mask, top, swap_lanes(low))
    q, e = encode(jnp.where(mask, swap_lanes(top), low))
    next_ref[pl.ds(pl.multiple_of(n * step, step), step), :] = q
    before = jnp.where(n == 0, 0, new[...])
    new[...] = jnp.where(row_is(new.shape, n), e, before)

    @pl.when(n == steps - 1)
    def _():
        next_ref[steps * step :, :] = new[...].astype(jnp.int16)


def relay_operands(gots, keeps):
    return [x for got, keep in zip(gots, keeps) for x in (got, got, got, keep, keep)]


def relay_specs(half, steps, at):
    step = half // 2 // steps
    top = pl.BlockSpec((step, LANES), lambda j: (at(j), 0))
    low = pl.BlockSpec((step, LANES), lambda j: (steps + at(j), 0))
    exps = pl.BlockSpec((PAD, LANES), lambda j: (half // PAD, 0))
    whole = pl.BlockSpec((half // 2 + PAD, LANES), lambda j: (0, 0))
    shapes = [
        jax.ShapeDtypeStruct((half // 2 + PAD, LANES), jnp.int16),
        jax.ShapeDtypeStruct((half // 2, LANES), f32),
    ]
    return [top, low, exps, top, low], [whole, top], shapes


def relay_kernel(tile, *refs):
    ins, outs, news = refs[:11], refs[11:15], refs[15:]
    n, steps = pl.program_id(0), pl.num_programs(0)
    for p in range(2):
        relay_step(n, steps, tile, ins[5 * p : 5 * p + 5], *outs[2 * p : 2 * p + 2], news[p])


def relay(gots, keeps, tile, dep):
    half = keeps[0].shape[0]
    steps = half // 2 // min(512, half // 2)
    ins, outs, shapes = relay_specs(half, steps, lambda j: j)
    return pl.pallas_call(
        functools.partial(relay_kernel, tile),
        grid=(steps,),
        in_specs=ins * 2 + [ANY],
        out_specs=outs * 2,
        out_shape=shapes * 2,
        scratch_shapes=[pltpu.VMEM((PAD, LANES), jnp.int32)] * 2,
        compiler_params=PARAMS,
        cost_estimate=LIGHT,
        name="relay",
    )(*relay_operands(gots, keeps), dep)


def inverse_norms(pieces_ref, k):
    x = pieces_ref[...].astype(f32)
    x = jnp.transpose(jnp.concatenate([x, x], axis=0))
    return (x[k : k + 1] + x[k + 4 : k + 5]) + x[k + 8 : k + 9]


def merged(op, x):
    return op(x, swap_lanes(x))


def summed(owns, lasts, inv, out_ref):
    top = None
    for p in range(2):
        packed = owns[p].shape[0]
        step = min(512, packed)
        exps = lasts[p][packed : packed + PAD, :].astype(jnp.int32)
        for n in range(packed // step):
            rows = slice(n * step, (n + 1) * step)
            x = owns[p][rows, :] + decode(lasts[p][rows, :], exps[n : n + 1, :])
            x = x * inv
            out_ref[p * packed + n * step : p * packed + (n + 1) * step, :] = x
            high = jnp.max(x, axis=0, keepdims=True)
            top = high if top is None else jnp.maximum(top, high)
    return merged(jnp.maximum, top)


def places(shape, at, packed):
    part, start = at // packed, at % packed
    row = lax.broadcasted_iota(jnp.int32, shape, 0) + (2 * part * packed + start)
    return jnp.where(low_lanes(shape), row, row + packed)


def student_kernel(k, op, oq, lp, lq, inv_ref, target_ref, base_ref, dep, out_ref, stats_ref):
    packed = op.shape[0]
    step = min(512, packed)
    top = summed((op, oq), (lp, lq), inverse_norms(inv_ref, k), out_ref)
    soft = jnp.zeros((1, LANES), f32)
    plain = jnp.zeros((1, LANES), f32)
    hit = jnp.zeros((1, LANES), f32)
    target = target_ref[...] - base_ref[0]
    for n in range(2 * packed // step):
        x = out_ref[n * step : (n + 1) * step, :]
        warm = jnp.exp((x - top) * (1.0 / heat))
        soft = soft + jnp.sum(warm, axis=0, keepdims=True)
        plain = plain + jnp.sum(warm * warm, axis=0, keepdims=True)
        here = places(x.shape, n * step, packed) == target
        hit = hit + jnp.sum(jnp.where(here, x, 0.0), axis=0, keepdims=True)
    stats = jnp.zeros((8, LANES), f32)
    sums = [merged(jnp.add, v) for v in (soft, plain, hit)]
    for n, value in enumerate([top] + sums):
        stats = jnp.where(row_is(stats.shape, n), value, stats)
    stats_ref[...] = stats


def teacher_kernel(k, op, oq, lp, lq, inv_ref, student_ref, before_ref, dep, out_ref, stats_ref):
    packed = op.shape[0]
    step = min(512, packed)
    top = summed((op, oq), (lp, lq), inverse_norms(inv_ref, k), out_ref)
    top = top * (1.0 / heat)
    total = jnp.zeros((1, LANES), f32)
    cross = jnp.zeros((1, LANES), f32)
    for n in range(2 * packed // step):
        rows = slice(n * step, (n + 1) * step)
        x = out_ref[rows, :]
        power = jnp.exp(x * (1.0 / heat) - top)
        total = total + jnp.sum(power, axis=0, keepdims=True)
        gap = (x - student_ref[rows, :]) * (1.0 / heat)
        cross = cross + jnp.sum(power * gap, axis=0, keepdims=True)
    stats = before_ref[...]
    sums = [merged(jnp.add, v) for v in (total, cross)]
    for n, value in enumerate([top] + sums):
        stats = jnp.where(row_is(stats.shape, 4 + n), value, stats)
    stats_ref[...] = stats


def finish(body, k, owns, lasts, inv, extra, dep):
    packed = owns[0].shape[0]
    last_spec = SMEM if body is student_kernel else VMEM
    return pl.pallas_call(
        functools.partial(body, k),
        in_specs=[VMEM] * 6 + [last_spec, ANY],
        out_specs=[VMEM] * 2,
        out_shape=[
            jax.ShapeDtypeStruct((2 * packed, LANES), f32),
            jax.ShapeDtypeStruct((8, LANES), f32),
        ],
        compiler_params=PARAMS,
        cost_estimate=LIGHT,
        name="finish",
    )(*owns, *lasts, inv, *extra, dep)


def tree_sum(parts):
    while len(parts) > 1:
        parts = [a + b for a, b in zip(parts[::2], parts[1::2])]
    return parts[0]


def thirds(x):
    high = x.astype(jnp.bfloat16).astype(f32)
    mid = (x - high).astype(jnp.bfloat16).astype(f32)
    return [high, mid, x - high - mid]


def slope_kernel(
    student_ref, teacher_ref, stats_ref, target_ref, base_ref, dep, grad_ref
):
    packed = student_ref.shape[0] // 2
    step = min(512, packed)
    sets = [stats_ref[k] for k in range(stats_ref.shape[0])]
    top = functools.reduce(jnp.maximum, sets)

    def scaled(row, top_row, rate):
        high = top[top_row : top_row + 1]
        return tree_sum(
            [s[row : row + 1] * jnp.exp((s[top_row : top_row + 1] - high) * rate) for s in sets]
        )

    student_top, teacher_top = top[0:1], top[4:5]
    soft_total = scaled(1, 0, 1.0 / heat)
    plain_total = scaled(2, 0, 1.0)
    teacher_total = scaled(5, 4, 1.0)
    cross_total = scaled(6, 4, 1.0)
    label = tree_sum([s[3:4] for s in sets])
    row_loss = blend * heat**2 * (
        cross_total / teacher_total
        - teacher_top
        - jnp.log(teacher_total)
        + student_top / heat
        + jnp.log(soft_total)
    ) + (1.0 - blend) * (student_top + jnp.log(plain_total) - label)
    soft_rate = grad_scale * blend * heat / soft_total
    teacher_rate = grad_scale * blend * heat / teacher_total
    plain_rate = grad_scale * (1.0 - blend) / plain_total
    inner = jnp.zeros((1, LANES), f32)
    target = target_ref[...] - base_ref[0]
    for n in range(2 * packed // step):
        rows = slice(n * step, (n + 1) * step)
        logits = student_ref[rows, :]
        warm = jnp.exp((logits - student_top) * (1.0 / heat))
        power = jnp.exp(teacher_ref[rows, :] * (1.0 / heat) - teacher_top)
        g = warm * (soft_rate + plain_rate * warm) - power * teacher_rate
        here = places(g.shape, n * step, packed) == target
        g = jnp.where(here, g - grad_scale * (1.0 - blend), g)
        g = g.astype(jnp.bfloat16).astype(f32)
        inner = inner + jnp.sum(g * logits, axis=0, keepdims=True)
        g = jnp.transpose(g).astype(jnp.bfloat16)
        at = 2 * (n * step // packed) * packed + (n * step) % packed
        grad_ref[:, at : at + step] = g[:QUARTER]
        grad_ref[:, at + packed : at + packed + step] = g[QUARTER:]
    extra = jnp.zeros((LANES, LANES), f32)
    for n, value in enumerate(thirds(merged(jnp.add, inner)) + thirds(row_loss)):
        extra = jnp.where(row_is(extra.shape, n), value, extra)
    extra = jnp.transpose(extra).astype(jnp.bfloat16)
    grad_ref[:, 2 * 2 * packed :] = extra[:QUARTER]


def slope(base, student, teacher, stats, targets, dep):
    return pl.pallas_call(
        slope_kernel,
        in_specs=[VMEM] * 4 + [SMEM, ANY],
        out_specs=VMEM,
        out_shape=jax.ShapeDtypeStruct((QUARTER, 2 * student.shape[0] + LANES), jnp.bfloat16),
        compiler_params=PARAMS,
        cost_estimate=LIGHT,
        name="slope",
    )(student, teacher, stats, targets, base, dep)


def norm_grad_kernel(t_ref, flip_ref, own, gx, gy, dp, dq, h_ref, dep, keep, send, loss, lhs):
    vocab, tile = h_ref.shape
    half = dp.shape[1]
    j = pl.program_id(0)
    t = jnp.bitwise_xor(t_ref[0], 2 * flip_ref[0])

    def place(n, columns, value):
        quarter = jnp.bitwise_xor(t, n)
        at = pl.ds(pl.multiple_of(lax.rem(quarter, 2) * QUARTER, QUARTER), QUARTER)

        @pl.when(quarter < 2)
        def _():
            keep[at, columns] = value

        @pl.when(quarter >= 2)
        def _():
            send[at, columns] = value

    @pl.when(j == 0)
    def _():
        for n, ref in enumerate((own, gx, gy)):
            lhs[n * QUARTER : (n + 1) * QUARTER, :] = ref[:, :vocab]
        lhs[3 * QUARTER :, :half] = dp[...]
        lhs[3 * QUARTER :, half:] = dq[:, : vocab - half]
        losses = []
        for n, ref in enumerate((own, gx, gy, dq)):
            x = ref[:, ref.shape[1] - LANES :].astype(f32)
            lane = lax.broadcasted_iota(jnp.int32, x.shape, 1)
            inner = jnp.sum(jnp.where(lane < 3, x, 0.0), axis=1, keepdims=True)
            place(n, slice(keep.shape[1] - LANES, keep.shape[1]), jnp.broadcast_to(inner, x.shape))
            x = jnp.where((lane >= 3) & (lane < 6), x, 0.0)
            losses.append(jnp.sum(jnp.sum(x, axis=1, keepdims=True), axis=0, keepdims=True))
        loss[...] = jnp.broadcast_to(tree_sum(losses), loss.shape)

    r = jnp.dot(lhs[...], h_ref[...], preferred_element_type=f32)
    columns = pl.ds(pl.multiple_of(j * tile, tile), tile)
    for n in range(4):
        place(n, columns, r[n * QUARTER : (n + 1) * QUARTER])


def norm_gradient(t, flip, own, gx, gy, dp, dq, head, dep):
    vocab, width = head.shape
    tile = min(512, width)
    parts = (own, gx, gy, dp, dq)
    rows = jax.ShapeDtypeStruct((2 * QUARTER, width + LANES), f32)
    return pl.pallas_call(
        norm_grad_kernel,
        grid=(width // tile,),
        in_specs=[SMEM, SMEM]
        + [pl.BlockSpec(x.shape, lambda j: (0, 0)) for x in parts]
        + [pl.BlockSpec((vocab, tile), lambda j: (0, j)), ANY],
        out_specs=[pl.BlockSpec(rows.shape, lambda j: (0, 0))] * 2
        + [pl.BlockSpec((8, LANES), lambda j: (0, 0))],
        out_shape=[rows, rows, jax.ShapeDtypeStruct((8, LANES), f32)],
        scratch_shapes=[pltpu.VMEM((4 * QUARTER, vocab), jnp.bfloat16)],
        compiler_params=PARAMS,
        cost_estimate=LIGHT,
        name="norm_grad",
    )(t, flip, *parts, head, dep)


def exponent(top):
    e = jnp.ceil(jnp.log2(jnp.maximum(top, 2.0**-44))).astype(jnp.int32)
    return jnp.clip(e, -44, 44)


def fold_kernel(z_ref, mine_ref, other_ref, dep_p, dep_q, own_ref, *sends):
    rows, width = own_ref.shape[0], own_ref.shape[1] - LANES
    for k in range(4):
        at = pl.ds(pl.multiple_of(jnp.bitwise_xor(z_ref[0], k) * rows, rows), rows)
        x = mine_ref[at, :] + other_ref[at, :]
        if k == 0:
            own_ref[...] = x
            continue
        norm, inner = x[:, :width], x[:, width:]
        e = exponent(jnp.max(jnp.abs(norm), axis=1, keepdims=True))
        q = jnp.clip(jnp.round(norm * pow2(15 - e)), -32767.0, 32767.0)
        sends[k - 1][:, :width] = q.astype(jnp.int32).astype(jnp.int16)
        e_inner = exponent(jnp.abs(inner))
        inner = jnp.clip(inner * pow2(15 - e_inner), -32767.0, 32767.0)
        high = jnp.round(inner)
        low = jnp.round((inner - high) * 32768.0)
        lane = lax.broadcasted_iota(jnp.int32, inner.shape, 1)
        tail = jnp.where(lane == 0, jnp.broadcast_to(e, inner.shape), e_inner)
        tail = jnp.where(lane == 2, high.astype(jnp.int32), tail)
        tail = jnp.where(lane == 3, low.astype(jnp.int32), tail)
        sends[k - 1][:, width:] = tail.astype(jnp.int16)


def fold(z, mine, other, deps):
    rows, width = other.shape
    return pl.pallas_call(
        fold_kernel,
        in_specs=[SMEM, VMEM, VMEM, ANY, ANY],
        out_specs=[VMEM] * 4,
        out_shape=[jax.ShapeDtypeStruct((rows // 4, width), f32)]
        + [jax.ShapeDtypeStruct((rows // 4, width), jnp.int16)] * 3,
        compiler_params=PARAMS,
        cost_estimate=LIGHT,
        name="fold",
    )(z, mine, other, *deps)


def last_kernel(features, own_ref, p1, p2, p3, hidden_ref, gain_ref, inv_ref, before, out_ref):
    width = hidden_ref.shape[1]
    norm, inner = own_ref[:, :width], own_ref[:, width : width + 1]
    for p in (p1, p2, p3):
        tail = p[:, width:].astype(jnp.int32)
        norm = norm + p[:, :width].astype(jnp.int32).astype(f32) * pow2(tail[:, 0:1] - 15)
        value = tail[:, 2:3].astype(f32) + tail[:, 3:4].astype(f32) * (1.0 / 32768.0)
        inner = inner + value * pow2(tail[:, 1:2] - 15)
    inv = inv_ref[:, :1]
    scale = inv * inv * inner * (1.0 / features)
    out = inv * gain_ref[...] * norm - hidden_ref[...].astype(f32) * scale
    out_ref[...] = out.astype(jnp.bfloat16)


def last(features, own, gots, hidden, gain, inv, part, before):
    count, width = own.shape[0], hidden.shape[1]
    block = pl.BlockSpec((count, width), lambda j: (part, 0))
    given = before is not None
    return pl.pallas_call(
        functools.partial(last_kernel, features),
        grid=(1,),
        in_specs=[VMEM] * 4
        + [block, VMEM, pl.BlockSpec((count, LANES), lambda j: (part, 0)), ANY],
        out_specs=block,
        out_shape=jax.ShapeDtypeStruct(hidden.shape, jnp.bfloat16),
        input_output_aliases={7: 0} if given else {},
        compiler_params=PARAMS,
        cost_estimate=LIGHT,
        name="hidden_grad",
    )(own, *gots, hidden, gain.reshape(1, -1), inv, before if given else inv)


def tie(x, *others):
    return lax.optimization_barrier((x, *others))[0]


def tok_sum(x):
    a = lax.ppermute(x, "tok", TOK_X)
    b = lax.ppermute(x, "tok", TOK_Y)
    c = lax.ppermute(x, "tok", TOK_D)
    return (x + a) + (b + c)


def small_box():
    return lax.axis_size("grp") == 2 and lax.axis_size("vocab") == 4


def along_z(x):
    return [x] + [lax.ppermute(x, "vocab", [(i, i ^ k) for i in range(4)]) for k in range(1, 4)]


def range_gather(x, ordered):
    if not small_box():
        return lax.all_gather(x, ("grp", "vocab"), axis=0)
    own = jnp.stack(along_z(x))
    sets = jnp.concatenate([own, lax.ppermute(own, "grp", SWAP)])
    if ordered:
        sets = sets[jnp.bitwise_xor(lax.axis_index(("grp", "vocab")), jnp.arange(8))]
    return sets


def on_device(
    teacher_hidden,
    student_hidden,
    teacher_gain,
    student_gain,
    teacher_head,
    student_head,
    target_ids,
):
    blocks = lax.axis_size("grp") * lax.axis_size("vocab")
    own_rows = teacher_hidden.shape[0]
    all_rows = blocks * own_rows
    part_rows = own_rows // 2
    vocab_local = teacher_head.shape[0]
    half = vocab_local // 2
    teacher_width = teacher_hidden.shape[1] * lax.axis_size("tok")
    student_width = student_hidden.shape[1] * lax.axis_size("tok")
    t = lax.axis_index("tok")
    t_arr = t.astype(jnp.int32).reshape(1)
    base = (lax.axis_index(("grp", "vocab")) * vocab_local).astype(jnp.int32).reshape(1)

    halves = [slice(0, part_rows), slice(part_rows, own_rows)]

    def gather_rows(x, after=None):
        if after is not None:
            x, _ = lax.optimization_barrier((x, after))
        return lax.all_gather(x, ("grp", "vocab"), axis=0, tiled=True)

    if small_box():
        near = along_z(student_hidden[halves[0]])
        sets = jnp.stack(near)
        sets = jnp.concatenate([sets, lax.ppermute(sets, "grp", SWAP)])
        place = jnp.bitwise_xor(lax.axis_index(("grp", "vocab")), jnp.arange(blocks))
        student_a = sets[place].reshape(blocks * part_rows, -1)
        first = near[1]
    else:
        student_a = gather_rows(student_hidden[halves[0]])
        first = student_a
    teacher_a = gather_rows(teacher_hidden[halves[0]], first)

    student_wide, teacher_wide, _ = lax.optimization_barrier(
        (student_hidden, teacher_hidden, first)
    )
    student_wide, teacher_wide = student_wide.astype(f32), teacher_wide.astype(f32)
    squares = jnp.stack(
        [jnp.sum(student_wide * student_wide, axis=1), jnp.sum(teacher_wide * teacher_wide, axis=1)]
    )
    squares = tok_sum(squares)
    widths = jnp.array([[student_width], [teacher_width]], f32)
    inverse = lax.rsqrt(squares / widths + epsilon)
    four = inverse.reshape(4, part_rows).T
    high = lax.reduce_precision(four, 8, 7)
    mid = lax.reduce_precision(four - high, 8, 7)
    pieces = jnp.concatenate([high, mid, four - high - mid], axis=1)
    pieces = jnp.pad(pieces, ((0, 0), (0, LANES - 12))).astype(jnp.bfloat16)
    student_b_own = jnp.concatenate([student_hidden[halves[1]], pieces], axis=1)
    targets = target_ids.reshape(blocks, own_rows)

    def mine(x):
        x = lax.dynamic_slice_in_dim(x, t * QUARTER, QUARTER)
        return jnp.concatenate([x, x]).reshape(1, LANES)

    def forward(next_p, own_p, next_q, own_q):
        last_p = lax.ppermute(next_p, "tok", TOK_Y)
        last_q = lax.ppermute(next_q, "tok", TOK_X)
        return (own_p, own_q), (last_p, last_q)

    def start(rows, gain, head, dep, pending=None):
        outs = partial_logits(t_arr, rows, gain, head, dep, pending)
        keep_p, send_p, keep_q, send_q, *passed = outs
        gots = (lax.ppermute(send_p, "tok", TOK_X), lax.ppermute(send_q, "tok", TOK_Y))
        unit = (gots, (keep_p, keep_q))
        return unit, (forward(*passed) if passed else None), keep_q

    def onward(unit, head, dep):
        outs = relay(*unit, logits_tile(head), dep)
        return (*forward(*outs), outs[3])

    def share(grad):
        return lax.ppermute(grad, "tok", TOK_X), lax.ppermute(grad, "tok", TOK_Y)

    def corners(grad, gx, gy):
        corner = (gx[:, :half], gy[:, half:])
        dp = lax.ppermute(corner[0], "tok", TOK_Y)
        dq = lax.ppermute(corner[1], "tok", TOK_X)
        return (grad, gx, gy, dp, dq), corner

    row_targets = [mine(targets[:, rows].reshape(-1)) for rows in halves]

    student, teacher = (student_gain, student_head), (teacher_gain, teacher_head)
    unit_sa, _, dep = start(student_a, *student, tie(base, *row_targets))
    student_b = gather_rows(student_b_own)
    teacher_b = gather_rows(teacher_hidden[halves[1]], dep)
    unit_ta, _, dep = start(teacher_a, *teacher, dep)
    unit_sb, sums_sa, dep = start(student_b, *student, dep, unit_sa)
    pieces = student_b[:, student_hidden.shape[1] :]
    pieces = lax.dynamic_slice_in_dim(pieces, t * QUARTER, QUARTER)
    unit_tb, sums_ta, dep = start(teacher_b, *teacher, tie(dep, pieces), unit_ta)
    logits_sa, stats = finish(
        student_kernel, 0, *sums_sa, pieces, (row_targets[0], base), dep
    )
    own_sb, last_sb, dep = onward(unit_sb, student_head, stats)
    own_tb, last_tb, dep = onward(unit_tb, teacher_head, dep)
    logits_ta, stats_a = finish(
        teacher_kernel, 2, *sums_ta, pieces, (logits_sa, stats), dep
    )
    all_a = range_gather(stats_a, False)
    grad_a = slope(base, logits_sa, logits_ta, all_a, row_targets[0], stats_a)
    gx_a, gy_a = share(grad_a)
    logits_sb, stats = finish(
        student_kernel, 1, own_sb, last_sb, pieces, (row_targets[1], base), grad_a
    )
    logits_tb, stats_b = finish(
        teacher_kernel, 3, own_tb, last_tb, pieces, (logits_sb, stats), stats
    )
    all_b = range_gather(stats_b, False)
    grad_b = slope(base, logits_sb, logits_tb, all_b, row_targets[1], stats_b)
    grads_a, corner = corners(grad_a, *lax.optimization_barrier((gx_a, gy_a, grad_b))[:2])
    gx_b, gy_b = share(tie(grad_b, *corner))
    grads_b, corner = corners(grad_b, gx_b, gy_b)

    own_inv = jnp.broadcast_to(inverse[0][:, None], (own_rows, LANES))
    flip = lax.axis_index("grp").astype(jnp.int32).reshape(1) * int(small_box())

    def result(grads, part, dep, fold_deps, before, arrived=()):
        mine, other, loss = norm_gradient(t_arr, flip, *grads, student_head, dep)
        if small_box():
            other = tie(other, *arrived)
            other = lax.ppermute(other, "grp", SWAP)
            z = lax.axis_index("vocab").astype(jnp.int32).reshape(1)
            own, *sends = fold(z, mine, other, fold_deps)
            gots = [
                lax.ppermute(x, "vocab", [(i, i ^ k) for i in range(4)])
                for k, x in enumerate(sends, 1)
            ]
            out = last(
                student_width, own, gots, student_hidden, student_gain, own_inv, part, before
            )
            return out, loss, own, gots
        norm = jnp.concatenate([mine, other])
        norm = lax.psum_scatter(norm, ("grp", "vocab"), scatter_dimension=0, tiled=True)
        at, width = halves[part], student_hidden.shape[1]
        inv, inner = own_inv[at, :1], norm[:, width : width + 1]
        out = inv * student_gain * norm[:, :width]
        out = out - student_hidden[at].astype(f32) * (inv * inv * inner / student_width)
        return out.astype(jnp.bfloat16), loss, mine, ()

    dep = tie(grad_b, own_inv)
    out, loss_a, dep, gots = result(grads_a, 0, dep, corner, None)
    second, loss_b, _, _ = result(grads_b, 1, dep, (t_arr, t_arr), out, gots)
    loss = (loss_a[0, 0] + loss_b[0, 0]) / all_rows
    return (loss, second if small_box() else jnp.concatenate([out, second]))


def solution(mesh):
    in_specs = (
        P(("grp", "vocab"), "tok"),
        P(("grp", "vocab"), "tok"),
        P("tok"),
        P("tok"),
        P(("grp", "vocab"), "tok"),
        P(("grp", "vocab"), "tok"),
        P(),
    )
    out_specs = (P(), P(("grp", "vocab"), "tok"))
    return jax.shard_map(
        on_device, mesh=mesh, in_specs=in_specs, out_specs=out_specs, check_vma=False
    )
```

```python
import functools
import jax
import jax.numpy as jnp
from jax import lax
from jax.experimental import pallas as pl
from jax.experimental.pallas import tpu as pltpu
from jax.sharding import PartitionSpec as P

heat = 2.0
blend = 0.5
grad_scale = 1024.0
epsilon = 1e-05

f32 = jnp.float32
VMEM_LIMIT = 56 * 1024 * 1024
LANES = 128
QUARTER = LANES // 2
PAD = 16
PIECE = 512

TOK_X = [(i, i ^ 1) for i in range(4)]
TOK_Y = [(i, i ^ 2) for i in range(4)]
TOK_D = [(i, i ^ 3) for i in range(4)]
SWAP = [(0, 1), (1, 0)]

VMEM = pl.BlockSpec(memory_space=pltpu.VMEM)
SMEM = pl.BlockSpec(memory_space=pltpu.SMEM)
ANY = pl.BlockSpec(memory_space=pl.ANY)
PARAMS = pltpu.CompilerParams(vmem_limit_bytes=VMEM_LIMIT)


LIGHT = pl.CostEstimate(flops=1024, bytes_accessed=1024, transcendentals=0)


def pow2(k):
    one = jnp.ones_like(k)
    a = jnp.left_shift(one, jnp.clip(k + 60, 0, 30)).astype(f32)
    b = jnp.left_shift(one, jnp.clip(k + 30, 0, 30)).astype(f32)
    c = jnp.left_shift(one, jnp.clip(k, 0, 30)).astype(f32)
    d = jnp.left_shift(one, jnp.clip(k - 30, 0, 30)).astype(f32)
    return (a * (2.0**-60)) * b * c * d


def encode(x):
    top = jnp.max(jnp.abs(x), axis=0, keepdims=True)
    e = jnp.ceil(jnp.log2(jnp.maximum(top, 2.0**-44))).astype(jnp.int32)
    e = jnp.clip(e, -44, 31)
    q = jnp.clip(jnp.round(x * pow2(15 - e)), -32767.0, 32767.0)
    return q.astype(jnp.int32).astype(jnp.int16), e


def decode(q, e):
    return q.astype(jnp.int32).astype(f32) * pow2(e - 15)


def low_lanes(shape):
    return lax.broadcasted_iota(jnp.int32, shape, 1) < QUARTER


def swap_lanes(x):
    return pltpu.roll(x, QUARTER, 1)


def row_is(shape, j):
    return lax.broadcasted_iota(jnp.int32, shape, 0) == j


ORDER = ((0, 2, 1, 3), (0, 1, 2, 3))


def logits_kernel(tiles, tile, relay_tile, t_ref, rows_ref, gain_ref, h_ref, dep_ref, *refs):
    passed = relay_tile is not None
    ins, refs = (refs[:10], refs[10:]) if passed else ((), refs)
    outs, refs = refs[:4], refs[4:]
    onward, refs = (refs[:4], refs[4:]) if passed else ((), refs)
    a_ref, exps, *news = refs
    j = pl.program_id(0)

    @pl.when(j == 0)
    def _():
        t = t_ref[0]
        for k in range(4):
            place = pl.multiple_of(jnp.bitwise_xor(t, k) * QUARTER, QUARTER)
            w = rows_ref[pl.ds(place, QUARTER), :].astype(f32) * gain_ref[...]
            w = w.astype(jnp.bfloat16)
            for part in range(2):
                at = ORDER[part].index(k) * QUARTER
                a_ref[part, at : at + QUARTER, :] = w

    for part in range(2):
        keep_ref, send_ref = outs[2 * part], outs[2 * part + 1]
        half = send_ref.shape[0] - PAD
        at = j - part * tiles

        @pl.when((at >= 0) & (at < tiles))
        def _():
            r = lax.dot_general(
                h_ref[...], a_ref[part], (((1,), (1,)), ((), ())), preferred_element_type=f32
            )
            if passed:
                relay_step(
                    at,
                    tiles,
                    relay_tile,
                    ins[5 * part : 5 * part + 5],
                    *onward[2 * part : 2 * part + 2],
                    news[part],
                )
            keep_ref[...] = r[:, :LANES]
            q, e = encode(r[:, LANES:])
            send_ref[pl.ds(pl.multiple_of(at * tile, tile), tile), :] = q
            before = jnp.where(at == 0, 0, exps[...])
            exps[...] = jnp.where(row_is((PAD, LANES), at), e, before)

            @pl.when(at == tiles - 1)
            def _():
                send_ref[half:, :] = exps[...].astype(jnp.int16)


def partial_logits(t, rows, gain, head, tile, dep, pending=None):
    count, width = rows.shape[0], head.shape[1]
    half = head.shape[0] // 2
    tiles = half // tile
    in_specs = [
        SMEM,
        pl.BlockSpec((count, width), lambda j: (0, 0)),
        pl.BlockSpec((1, width), lambda j: (0, 0)),
        pl.BlockSpec((tile, width), lambda j: (j, 0)),
        ANY,
    ]
    out_specs, out_shape, operands, extra = [], [], [], []
    ats = [lambda j, part=part: jnp.clip(j - part * tiles, 0, tiles - 1) for part in range(2)]
    for at in ats:
        out_specs += [
            pl.BlockSpec((tile, LANES), lambda j, at=at: (at(j), 0)),
            pl.BlockSpec((half + PAD, LANES), lambda j: (0, 0)),
        ]
        out_shape += [
            jax.ShapeDtypeStruct((half, LANES), f32),
            jax.ShapeDtypeStruct((half + PAD, LANES), jnp.int16),
        ]
    if pending is not None:
        operands = relay_operands(*pending[:2])
        extra = [pltpu.VMEM((PAD, LANES), jnp.int32)] * 2
        for at in ats:
            ins, outs, shapes = relay_specs(half, tiles, at)
            in_specs += ins
            out_specs += outs
            out_shape += shapes
    return pl.pallas_call(
        functools.partial(logits_kernel, tiles, tile, pending and pending[2]),
        grid=(2 * tiles,),
        in_specs=in_specs,
        out_specs=out_specs,
        out_shape=out_shape,
        scratch_shapes=[
            pltpu.VMEM((2, count, width), jnp.bfloat16),
            pltpu.VMEM((PAD, LANES), jnp.int32),
            *extra,
        ],
        compiler_params=PARAMS,
        cost_estimate=LIGHT,
        name="logits",
    )(t, rows, gain.reshape(1, width), head, dep, *operands)


def relay_step(n, steps, tile, ins, next_ref, own_ref, new):
    got_top, got_low, exps_ref, keep_top, keep_low = ins
    step = own_ref.shape[0]
    exps = exps_ref[...].astype(jnp.int32)

    def exponent_at(at):
        here = row_is(exps.shape, at // tile)
        return jnp.sum(jnp.where(here, exps, 0), axis=0, keepdims=True)

    top = keep_top[...] + decode(got_top[...], exponent_at(n * step))
    low = keep_low[...] + decode(got_low[...], exponent_at((steps + n) * step))
    mask = low_lanes(top.shape)
    own_ref[...] = jnp.where(mask, top, swap_lanes(low))
    q, e = encode(jnp.where(mask, swap_lanes(top), low))
    next_ref[pl.ds(pl.multiple_of(n * step, step), step), :] = q
    pieces = step // min(PIECE, steps * step)
    before = jnp.where(n == 0, 0, new[...])
    row = lax.broadcasted_iota(jnp.int32, new.shape, 0)
    here = (row >= n * pieces) & (row < (n + 1) * pieces)
    new[...] = jnp.where(here, e, before)

    @pl.when(n == steps - 1)
    def _():
        next_ref[steps * step :, :] = new[...].astype(jnp.int16)


def relay_operands(gots, keeps):
    return [x for got, keep in zip(gots, keeps) for x in (got, got, got, keep, keep)]


def relay_specs(half, steps, at):
    step = half // 2 // steps
    top = pl.BlockSpec((step, LANES), lambda j: (at(j), 0))
    low = pl.BlockSpec((step, LANES), lambda j: (steps + at(j), 0))
    exps = pl.BlockSpec((PAD, LANES), lambda j: (half // PAD, 0))
    whole = pl.BlockSpec((half // 2 + PAD, LANES), lambda j: (0, 0))
    shapes = [
        jax.ShapeDtypeStruct((half // 2 + PAD, LANES), jnp.int16),
        jax.ShapeDtypeStruct((half // 2, LANES), f32),
    ]
    return [top, low, exps, top, low], [whole, top], shapes


def relay_kernel(tile, *refs):
    ins, outs, news = refs[:11], refs[11:15], refs[15:]
    n, steps = pl.program_id(0), pl.num_programs(0)
    for p in range(2):
        relay_step(n, steps, tile, ins[5 * p : 5 * p + 5], *outs[2 * p : 2 * p + 2], news[p])


def relay(gots, keeps, tile, dep):
    half = keeps[0].shape[0]
    steps = half // 2 // min(PIECE, half // 2)
    ins, outs, shapes = relay_specs(half, steps, lambda j: j)
    return pl.pallas_call(
        functools.partial(relay_kernel, tile),
        grid=(steps,),
        in_specs=ins * 2 + [ANY],
        out_specs=outs * 2,
        out_shape=shapes * 2,
        scratch_shapes=[pltpu.VMEM((PAD, LANES), jnp.int32)] * 2,
        compiler_params=PARAMS,
        cost_estimate=LIGHT,
        name="relay",
    )(*relay_operands(gots, keeps), dep)


def inverse_norms(pieces_ref, k):
    x = pieces_ref[...].astype(f32)
    x = jnp.transpose(jnp.concatenate([x, x], axis=0))
    return (x[k : k + 1] + x[k + 4 : k + 5]) + x[k + 8 : k + 9]


def merged(op, x):
    return op(x, swap_lanes(x))


def summed(owns, lasts, inv, out_ref):
    top = None
    for p in range(2):
        packed = owns[p].shape[0]
        step = min(PIECE, packed)
        exps = lasts[p][packed : packed + PAD, :].astype(jnp.int32)
        for n in range(packed // step):
            rows = slice(n * step, (n + 1) * step)
            x = owns[p][rows, :] + decode(lasts[p][rows, :], exps[n : n + 1, :])
            x = x * inv
            out_ref[p * packed + n * step : p * packed + (n + 1) * step, :] = x
            high = jnp.max(x, axis=0, keepdims=True)
            top = high if top is None else jnp.maximum(top, high)
    return merged(jnp.maximum, top)


def places(shape, at, packed):
    part, start = at // packed, at % packed
    row = lax.broadcasted_iota(jnp.int32, shape, 0) + (2 * part * packed + start)
    return jnp.where(low_lanes(shape), row, row + packed)


def student_kernel(k, op, oq, lp, lq, inv_ref, target_ref, base_ref, dep, out_ref, stats_ref):
    packed = op.shape[0]
    step = min(512, packed)
    top = summed((op, oq), (lp, lq), inverse_norms(inv_ref, k), out_ref)
    soft = jnp.zeros((1, LANES), f32)
    plain = jnp.zeros((1, LANES), f32)
    hit = jnp.zeros((1, LANES), f32)
    target = target_ref[...] - base_ref[0]
    for n in range(2 * packed // step):
        x = out_ref[n * step : (n + 1) * step, :]
        warm = jnp.exp((x - top) * (1.0 / heat))
        soft = soft + jnp.sum(warm, axis=0, keepdims=True)
        plain = plain + jnp.sum(warm * warm, axis=0, keepdims=True)
        here = places(x.shape, n * step, packed) == target
        hit = hit + jnp.sum(jnp.where(here, x, 0.0), axis=0, keepdims=True)
    stats = jnp.zeros((8, LANES), f32)
    sums = [merged(jnp.add, v) for v in (soft, plain, hit)]
    for n, value in enumerate([top] + sums):
        stats = jnp.where(row_is(stats.shape, n), value, stats)
    stats_ref[...] = stats


def teacher_kernel(k, op, oq, lp, lq, inv_ref, student_ref, before_ref, dep, out_ref, stats_ref):
    packed = op.shape[0]
    step = min(512, packed)
    top = summed((op, oq), (lp, lq), inverse_norms(inv_ref, k), out_ref)
    top = top * (1.0 / heat)
    total = jnp.zeros((1, LANES), f32)
    cross = jnp.zeros((1, LANES), f32)
    for n in range(2 * packed // step):
        rows = slice(n * step, (n + 1) * step)
        x = out_ref[rows, :]
        power = jnp.exp(x * (1.0 / heat) - top)
        total = total + jnp.sum(power, axis=0, keepdims=True)
        gap = (x - student_ref[rows, :]) * (1.0 / heat)
        cross = cross + jnp.sum(power * gap, axis=0, keepdims=True)
    stats = before_ref[...]
    sums = [merged(jnp.add, v) for v in (total, cross)]
    for n, value in enumerate([top] + sums):
        stats = jnp.where(row_is(stats.shape, 4 + n), value, stats)
    stats_ref[...] = stats


def finish(body, k, owns, lasts, inv, extra, dep):
    packed = owns[0].shape[0]
    last_spec = SMEM if body is student_kernel else VMEM
    return pl.pallas_call(
        functools.partial(body, k),
        in_specs=[VMEM] * 6 + [last_spec, ANY],
        out_specs=[VMEM] * 2,
        out_shape=[
            jax.ShapeDtypeStruct((2 * packed, LANES), f32),
            jax.ShapeDtypeStruct((8, LANES), f32),
        ],
        compiler_params=PARAMS,
        cost_estimate=LIGHT,
        name="finish",
    )(*owns, *lasts, inv, *extra, dep)


def tree_sum(parts):
    while len(parts) > 1:
        parts = [a + b for a, b in zip(parts[::2], parts[1::2])]
    return parts[0]


def thirds(x):
    high = x.astype(jnp.bfloat16).astype(f32)
    mid = (x - high).astype(jnp.bfloat16).astype(f32)
    return [high, mid, x - high - mid]


def slope_kernel(
    student_ref, teacher_ref, stats_ref, target_ref, base_ref, dep, grad_ref
):
    packed = student_ref.shape[0] // 2
    step = min(512, packed)
    sets = [stats_ref[k] for k in range(stats_ref.shape[0])]
    top = functools.reduce(jnp.maximum, sets)

    def scaled(row, top_row, rate):
        high = top[top_row : top_row + 1]
        return tree_sum(
            [s[row : row + 1] * jnp.exp((s[top_row : top_row + 1] - high) * rate) for s in sets]
        )

    student_top, teacher_top = top[0:1], top[4:5]
    soft_total = scaled(1, 0, 1.0 / heat)
    plain_total = scaled(2, 0, 1.0)
    teacher_total = scaled(5, 4, 1.0)
    cross_total = scaled(6, 4, 1.0)
    label = tree_sum([s[3:4] for s in sets])
    row_loss = blend * heat**2 * (
        cross_total / teacher_total
        - teacher_top
        - jnp.log(teacher_total)
        + student_top / heat
        + jnp.log(soft_total)
    ) + (1.0 - blend) * (student_top + jnp.log(plain_total) - label)
    soft_rate = grad_scale * blend * heat / soft_total
    teacher_rate = grad_scale * blend * heat / teacher_total
    plain_rate = grad_scale * (1.0 - blend) / plain_total
    inner = jnp.zeros((1, LANES), f32)
    target = target_ref[...] - base_ref[0]
    for n in range(2 * packed // step):
        rows = slice(n * step, (n + 1) * step)
        logits = student_ref[rows, :]
        warm = jnp.exp((logits - student_top) * (1.0 / heat))
        power = jnp.exp(teacher_ref[rows, :] * (1.0 / heat) - teacher_top)
        g = warm * (soft_rate + plain_rate * warm) - power * teacher_rate
        here = places(g.shape, n * step, packed) == target
        g = jnp.where(here, g - grad_scale * (1.0 - blend), g)
        g = g.astype(jnp.bfloat16).astype(f32)
        inner = inner + jnp.sum(g * logits, axis=0, keepdims=True)
        g = jnp.transpose(g).astype(jnp.bfloat16)
        at = 2 * (n * step // packed) * packed + (n * step) % packed
        grad_ref[:, at : at + step] = g[:QUARTER]
        grad_ref[:, at + packed : at + packed + step] = g[QUARTER:]
    extra = jnp.zeros((LANES, LANES), f32)
    for n, value in enumerate(thirds(merged(jnp.add, inner)) + thirds(row_loss)):
        extra = jnp.where(row_is(extra.shape, n), value, extra)
    extra = jnp.transpose(extra).astype(jnp.bfloat16)
    grad_ref[:, 2 * 2 * packed :] = extra[:QUARTER]


def slope(base, student, teacher, stats, targets, dep):
    return pl.pallas_call(
        slope_kernel,
        in_specs=[VMEM] * 4 + [SMEM, ANY],
        out_specs=VMEM,
        out_shape=jax.ShapeDtypeStruct((QUARTER, 2 * student.shape[0] + LANES), jnp.bfloat16),
        compiler_params=PARAMS,
        cost_estimate=LIGHT,
        name="slope",
    )(student, teacher, stats, targets, base, dep)


def norm_grad_kernel(t_ref, flip_ref, own, gx, gy, dp, dq, h_ref, dep, keep, send, loss, lhs):
    vocab, tile = h_ref.shape
    half = dp.shape[1]
    j = pl.program_id(0)
    t = jnp.bitwise_xor(t_ref[0], 2 * flip_ref[0])

    def place(n, columns, value):
        quarter = jnp.bitwise_xor(t, n)
        at = pl.ds(pl.multiple_of(lax.rem(quarter, 2) * QUARTER, QUARTER), QUARTER)

        @pl.when(quarter < 2)
        def _():
            keep[at, columns] = value

        @pl.when(quarter >= 2)
        def _():
            send[at, columns] = value

    @pl.when(j == 0)
    def _():
        for n, ref in enumerate((own, gx, gy)):
            lhs[n * QUARTER : (n + 1) * QUARTER, :] = ref[:, :vocab]
        lhs[3 * QUARTER :, :half] = dp[...]
        lhs[3 * QUARTER :, half:] = dq[:, : vocab - half]
        losses = []
        for n, ref in enumerate((own, gx, gy, dq)):
            x = ref[:, ref.shape[1] - LANES :].astype(f32)
            lane = lax.broadcasted_iota(jnp.int32, x.shape, 1)
            inner = jnp.sum(jnp.where(lane < 3, x, 0.0), axis=1, keepdims=True)
            place(n, slice(keep.shape[1] - LANES, keep.shape[1]), jnp.broadcast_to(inner, x.shape))
            x = jnp.where((lane >= 3) & (lane < 6), x, 0.0)
            losses.append(jnp.sum(jnp.sum(x, axis=1, keepdims=True), axis=0, keepdims=True))
        loss[...] = jnp.broadcast_to(tree_sum(losses), loss.shape)

    r = jnp.dot(lhs[...], h_ref[...], preferred_element_type=f32)
    columns = pl.ds(pl.multiple_of(j * tile, tile), tile)
    for n in range(4):
        place(n, columns, r[n * QUARTER : (n + 1) * QUARTER])


def norm_gradient(t, flip, own, gx, gy, dp, dq, head, dep):
    vocab, width = head.shape
    tile = min(512, width)
    parts = (own, gx, gy, dp, dq)
    rows = jax.ShapeDtypeStruct((2 * QUARTER, width + LANES), f32)
    return pl.pallas_call(
        norm_grad_kernel,
        grid=(width // tile,),
        in_specs=[SMEM, SMEM]
        + [pl.BlockSpec(x.shape, lambda j: (0, 0)) for x in parts]
        + [pl.BlockSpec((vocab, tile), lambda j: (0, j)), ANY],
        out_specs=[pl.BlockSpec(rows.shape, lambda j: (0, 0))] * 2
        + [pl.BlockSpec((8, LANES), lambda j: (0, 0))],
        out_shape=[rows, rows, jax.ShapeDtypeStruct((8, LANES), f32)],
        scratch_shapes=[pltpu.VMEM((4 * QUARTER, vocab), jnp.bfloat16)],
        compiler_params=PARAMS,
        cost_estimate=LIGHT,
        name="norm_grad",
    )(t, flip, *parts, head, dep)


def exponent(top):
    e = jnp.ceil(jnp.log2(jnp.maximum(top, 2.0**-44))).astype(jnp.int32)
    return jnp.clip(e, -44, 44)


def fold_kernel(z_ref, mine_ref, other_ref, dep_p, dep_q, own_ref, *sends):
    rows, width = own_ref.shape[0], own_ref.shape[1] - LANES
    for k in range(4):
        at = pl.ds(pl.multiple_of(jnp.bitwise_xor(z_ref[0], k) * rows, rows), rows)
        x = mine_ref[at, :] + other_ref[at, :]
        if k == 0:
            own_ref[...] = x
            continue
        norm, inner = x[:, :width], x[:, width:]
        e = exponent(jnp.max(jnp.abs(norm), axis=1, keepdims=True))
        q = jnp.clip(jnp.round(norm * pow2(15 - e)), -32767.0, 32767.0)
        sends[k - 1][:, :width] = q.astype(jnp.int32).astype(jnp.int16)
        e_inner = exponent(jnp.abs(inner))
        inner = jnp.clip(inner * pow2(15 - e_inner), -32767.0, 32767.0)
        high = jnp.round(inner)
        low = jnp.round((inner - high) * 32768.0)
        lane = lax.broadcasted_iota(jnp.int32, inner.shape, 1)
        tail = jnp.where(lane == 0, jnp.broadcast_to(e, inner.shape), e_inner)
        tail = jnp.where(lane == 2, high.astype(jnp.int32), tail)
        tail = jnp.where(lane == 3, low.astype(jnp.int32), tail)
        sends[k - 1][:, width:] = tail.astype(jnp.int16)


def fold(z, mine, other, deps):
    rows, width = other.shape
    return pl.pallas_call(
        fold_kernel,
        in_specs=[SMEM, VMEM, VMEM, ANY, ANY],
        out_specs=[VMEM] * 4,
        out_shape=[jax.ShapeDtypeStruct((rows // 4, width), f32)]
        + [jax.ShapeDtypeStruct((rows // 4, width), jnp.int16)] * 3,
        compiler_params=PARAMS,
        cost_estimate=LIGHT,
        name="fold",
    )(z, mine, other, *deps)


def last_kernel(features, own_ref, p1, p2, p3, hidden_ref, gain_ref, inv_ref, before, out_ref):
    width = hidden_ref.shape[1]
    norm, inner = own_ref[:, :width], own_ref[:, width : width + 1]
    for p in (p1, p2, p3):
        tail = p[:, width:].astype(jnp.int32)
        norm = norm + p[:, :width].astype(jnp.int32).astype(f32) * pow2(tail[:, 0:1] - 15)
        value = tail[:, 2:3].astype(f32) + tail[:, 3:4].astype(f32) * (1.0 / 32768.0)
        inner = inner + value * pow2(tail[:, 1:2] - 15)
    inv = inv_ref[:, :1]
    scale = inv * inv * inner * (1.0 / features)
    out = inv * gain_ref[...] * norm - hidden_ref[...].astype(f32) * scale
    out_ref[...] = out.astype(jnp.bfloat16)


def last(features, own, gots, hidden, gain, inv, part, before):
    count, width = own.shape[0], hidden.shape[1]
    block = pl.BlockSpec((count, width), lambda j: (part, 0))
    given = before is not None
    return pl.pallas_call(
        functools.partial(last_kernel, features),
        grid=(1,),
        in_specs=[VMEM] * 4
        + [block, VMEM, pl.BlockSpec((count, LANES), lambda j: (part, 0)), ANY],
        out_specs=block,
        out_shape=jax.ShapeDtypeStruct(hidden.shape, jnp.bfloat16),
        input_output_aliases={7: 0} if given else {},
        compiler_params=PARAMS,
        cost_estimate=LIGHT,
        name="hidden_grad",
    )(own, *gots, hidden, gain.reshape(1, -1), inv, before if given else inv)


def tie(x, *others):
    return lax.optimization_barrier((x, *others))[0]


def tok_sum(x):
    a = lax.ppermute(x, "tok", TOK_X)
    b = lax.ppermute(x, "tok", TOK_Y)
    c = lax.ppermute(x, "tok", TOK_D)
    return (x + a) + (b + c)


def small_box():
    return lax.axis_size("grp") == 2 and lax.axis_size("vocab") == 4


def along_z(x):
    return [x] + [lax.ppermute(x, "vocab", [(i, i ^ k) for i in range(4)]) for k in range(1, 4)]


def range_gather(x, ordered):
    if not small_box():
        return lax.all_gather(x, ("grp", "vocab"), axis=0)
    own = jnp.stack(along_z(x))
    sets = jnp.concatenate([own, lax.ppermute(own, "grp", SWAP)])
    if ordered:
        sets = sets[jnp.bitwise_xor(lax.axis_index(("grp", "vocab")), jnp.arange(8))]
    return sets


def on_device(
    teacher_hidden,
    student_hidden,
    teacher_gain,
    student_gain,
    teacher_head,
    student_head,
    target_ids,
):
    blocks = lax.axis_size("grp") * lax.axis_size("vocab")
    own_rows = teacher_hidden.shape[0]
    all_rows = blocks * own_rows
    part_rows = own_rows // 2
    vocab_local = teacher_head.shape[0]
    half = vocab_local // 2
    teacher_width = teacher_hidden.shape[1] * lax.axis_size("tok")
    student_width = student_hidden.shape[1] * lax.axis_size("tok")
    t = lax.axis_index("tok")
    t_arr = t.astype(jnp.int32).reshape(1)
    base = (lax.axis_index(("grp", "vocab")) * vocab_local).astype(jnp.int32).reshape(1)

    halves = [slice(0, part_rows), slice(part_rows, own_rows)]

    def gather_rows(x, after=None):
        if after is not None:
            x, _ = lax.optimization_barrier((x, after))
        return lax.all_gather(x, ("grp", "vocab"), axis=0, tiled=True)

    if small_box():
        near = along_z(student_hidden[halves[0]])
        sets = jnp.stack(near)
        sets = jnp.concatenate([sets, lax.ppermute(sets, "grp", SWAP)])
        place = jnp.bitwise_xor(lax.axis_index(("grp", "vocab")), jnp.arange(blocks))
        student_a = sets[place].reshape(blocks * part_rows, -1)
        first = near[1]
    else:
        student_a = gather_rows(student_hidden[halves[0]])
        first = student_a
    teacher_a = gather_rows(teacher_hidden[halves[0]], first)

    student_wide, teacher_wide, _ = lax.optimization_barrier(
        (student_hidden, teacher_hidden, first)
    )
    student_wide, teacher_wide = student_wide.astype(f32), teacher_wide.astype(f32)
    squares = jnp.stack(
        [jnp.sum(student_wide * student_wide, axis=1), jnp.sum(teacher_wide * teacher_wide, axis=1)]
    )
    squares = tok_sum(squares)
    widths = jnp.array([[student_width], [teacher_width]], f32)
    inverse = lax.rsqrt(squares / widths + epsilon)
    four = inverse.reshape(4, part_rows).T
    high = lax.reduce_precision(four, 8, 7)
    mid = lax.reduce_precision(four - high, 8, 7)
    pieces = jnp.concatenate([high, mid, four - high - mid], axis=1)
    pieces = jnp.pad(pieces, ((0, 0), (0, LANES - 12))).astype(jnp.bfloat16)
    student_b_own = jnp.concatenate([student_hidden[halves[1]], pieces], axis=1)
    targets = target_ids.reshape(blocks, own_rows)

    def mine(x):
        x = lax.dynamic_slice_in_dim(x, t * QUARTER, QUARTER)
        return jnp.concatenate([x, x]).reshape(1, LANES)

    def forward(next_p, own_p, next_q, own_q):
        last_p = lax.ppermute(next_p, "tok", TOK_Y)
        last_q = lax.ppermute(next_q, "tok", TOK_X)
        return (own_p, own_q), (last_p, last_q)

    def start(rows, gain, head, dep, pending=None, tile=1024):
        tile = min(tile, half)
        outs = partial_logits(t_arr, rows, gain, head, tile, dep, pending)
        keep_p, send_p, keep_q, send_q, *passed = outs
        gots = (lax.ppermute(send_p, "tok", TOK_X), lax.ppermute(send_q, "tok", TOK_Y))
        unit = (gots, (keep_p, keep_q), tile)
        return unit, (forward(*passed) if passed else None), keep_q

    def onward(unit, dep):
        outs = relay(*unit, dep)
        return (*forward(*outs), outs[3])

    def share(grad):
        return lax.ppermute(grad, "tok", TOK_X), lax.ppermute(grad, "tok", TOK_Y)

    def corners(grad, gx, gy):
        corner = (gx[:, :half], gy[:, half:])
        dp = lax.ppermute(corner[0], "tok", TOK_Y)
        dq = lax.ppermute(corner[1], "tok", TOK_X)
        return (grad, gx, gy, dp, dq), corner

    row_targets = [mine(targets[:, rows].reshape(-1)) for rows in halves]

    student, teacher = (student_gain, student_head), (teacher_gain, teacher_head)
    unit_sa, _, dep = start(student_a, *student, tie(base, *row_targets), tile=2048)
    student_b = gather_rows(student_b_own, dep)
    teacher_b = gather_rows(teacher_hidden[halves[1]], dep)
    unit_ta, _, dep = start(teacher_a, *teacher, dep)
    unit_sb, sums_sa, dep = start(student_b, *student, dep, unit_sa, tile=2048)
    pieces = student_b[:, student_hidden.shape[1] :]
    pieces = lax.dynamic_slice_in_dim(pieces, t * QUARTER, QUARTER)
    unit_tb, sums_ta, dep = start(teacher_b, *teacher, tie(dep, pieces), unit_ta)
    logits_sa, stats = finish(
        student_kernel, 0, *sums_sa, pieces, (row_targets[0], base), dep
    )
    own_sb, last_sb, dep = onward(unit_sb, stats)
    logits_ta, stats_a = finish(
        teacher_kernel, 2, *sums_ta, pieces, (logits_sa, stats), dep
    )
    all_a = range_gather(stats_a, False)
    own_tb, last_tb, dep = onward(unit_tb, stats_a)
    grad_a = slope(base, logits_sa, logits_ta, all_a, row_targets[0], dep)
    gx_a, gy_a = share(grad_a)
    logits_sb, stats = finish(
        student_kernel, 1, own_sb, last_sb, pieces, (row_targets[1], base), grad_a
    )
    logits_tb, stats_b = finish(
        teacher_kernel, 3, own_tb, last_tb, pieces, (logits_sb, stats), stats
    )
    all_b = range_gather(stats_b, False)
    grad_b = slope(base, logits_sb, logits_tb, all_b, row_targets[1], stats_b)
    grads_a, corner = corners(grad_a, gx_a, gy_a)
    gx_b, gy_b = share(tie(grad_b, *corner))
    grads_b, corner = corners(grad_b, gx_b, gy_b)

    own_inv = jnp.broadcast_to(inverse[0][:, None], (own_rows, LANES))
    flip = lax.axis_index("grp").astype(jnp.int32).reshape(1) * int(small_box())

    def result(grads, part, dep, fold_deps, before, arrived=()):
        mine, other, loss = norm_gradient(t_arr, flip, *grads, student_head, dep)
        if small_box():
            other = tie(other, *arrived)
            other = lax.ppermute(other, "grp", SWAP)
            z = lax.axis_index("vocab").astype(jnp.int32).reshape(1)
            own, *sends = fold(z, mine, other, fold_deps)
            gots = [
                lax.ppermute(x, "vocab", [(i, i ^ k) for i in range(4)])
                for k, x in enumerate(sends, 1)
            ]
            out = last(
                student_width, own, gots, student_hidden, student_gain, own_inv, part, before
            )
            return out, loss, own, gots
        norm = jnp.concatenate([mine, other])
        norm = lax.psum_scatter(norm, ("grp", "vocab"), scatter_dimension=0, tiled=True)
        at, width = halves[part], student_hidden.shape[1]
        inv, inner = own_inv[at, :1], norm[:, width : width + 1]
        out = inv * student_gain * norm[:, :width]
        out = out - student_hidden[at].astype(f32) * (inv * inv * inner / student_width)
        return out.astype(jnp.bfloat16), loss, mine, ()

    dep = tie(grad_b, own_inv)
    out, loss_a, dep, gots = result(grads_a, 0, dep, corner, None)
    second, loss_b, _, _ = result(grads_b, 1, dep, (t_arr, t_arr), out, gots)
    loss = (loss_a[0, 0] + loss_b[0, 0]) / all_rows
    return (loss, second if small_box() else jnp.concatenate([out, second]))


def solution(mesh):
    in_specs = (
        P(("grp", "vocab"), "tok"),
        P(("grp", "vocab"), "tok"),
        P("tok"),
        P("tok"),
        P(("grp", "vocab"), "tok"),
        P(("grp", "vocab"), "tok"),
        P(),
    )
    out_specs = (P(), P(("grp", "vocab"), "tok"))
    return jax.shard_map(
        on_device, mesh=mesh, in_specs=in_specs, out_specs=out_specs, check_vma=False
    )
```
